32 devices in a mesh: gx: 8 (over y, x, core), gy: 4 (over z).
Axes of the slice: x: 2, y: 2, z: 4, core: 2. Of those that a mesh axis runs over, the one named last changes fastest.
Arguments:
- load: float32 [8, 4, 96, 896], P('gx', 'gy'), may hold values from -80 to 80
- dual_operator: bfloat16 [8, 4, 896, 896], P('gx', 'gy'), may hold values from -1 to 2
- dirichlet: bfloat16 [8, 4, 896, 896], P('gx', 'gy'), may hold values from -1 to 2
- modes: bfloat16 [8, 4, 12, 896], P('gx', 'gy'), may hold values from -1 to 1
- coarse_inverse: float32 [8, 48, 4, 96], P('gx', None, 'gy'), may hold values from -1 to 2, as said below
- face_counts: int32 [8, 4, 4], P('gx', 'gy'), may hold values from 0 to 224, as said below
- partners: int32 [8, 4, 4, 224], P('gx', 'gy'), may hold values from 0 to 223, as said below
Outputs:
- multipliers: float32 [8, 4, 96, 896], P('gx', 'gy')
- residual: float32 [8, 4, 96, 896], P('gx', 'gy')
The draws below stay inside these ranges and needn't reach their ends.
Inputs may be any that keep to these rules, and one draw needn't show every extreme that they name: `face_counts`: the two faces of one interface have equal counts; faces on the grid's outer boundary have 0; every other face has at least half of 224; some face has exactly 224. `partners`: each face's list is a permutation of the slots that maps the live slots onto the live slots of the neighbour's facing face; the facing face's list is its inverse. `coarse_inverse`: the coarse inverse is symmetric: the entry of coefficients u, v equals that of v, u.
All inputs are finite; a program needn't handle non-finite values.
Results may differ from the reference program's by a relative error of at most 0.00365.
The reference program's roundings to bfloat16 on the way count: a program that leaves them out, or rounds other values in their place, can miss the bound.
Values may be sent and summed in bfloat16 or wider, within the bound.
No kernel may reach another device: no remote copies, remote signals or barrier semaphores. Data moves between devices by JAX's collectives and lax.ppermute only.
A program may use at most 64 MiB of HBM per device.

```python
import jax
import jax.numpy as jnp
from jax import lax

FACE_SLOTS = 224
MULTIPLIERS = 896
LOAD_COLUMNS = 96
COARSE_MODES = 12
ITERATIONS = 2
SUBDOMAIN_ROWS = 8
SUBDOMAIN_COLS = 4
COARSE_SIZE = 384


def clipped_noise(noise_key, shape):
    return jnp.clip(jax.random.normal(noise_key, shape, jnp.float32), -4.0, 4.0)


def coarse_basis(key):
    basis_key = jax.random.fold_in(key, 21)
    random_part = clipped_noise(basis_key, (SUBDOMAIN_ROWS, SUBDOMAIN_COLS, COARSE_MODES, MULTIPLIERS))
    return (random_part / jnp.sqrt(jnp.float32(MULTIPLIERS))).astype(jnp.bfloat16)


def draw_modes(key, part):
    return coarse_basis(key)


def draw_load(key, part):
    mode_rows = coarse_basis(key).astype(jnp.float32)
    weights = 3.0 * clipped_noise(jax.random.fold_in(key, 22), (SUBDOMAIN_ROWS, SUBDOMAIN_COLS, LOAD_COLUMNS, COARSE_MODES))
    random_part = clipped_noise(jax.random.fold_in(key, 23), (SUBDOMAIN_ROWS, SUBDOMAIN_COLS, LOAD_COLUMNS, MULTIPLIERS))
    return random_part + jnp.einsum('abrk,abkm->abrm', weights, mode_rows)


def dense_operator(key, salt_value):
    salted = jax.random.fold_in(key, salt_value)
    diag_key, noise_key = jax.random.split(salted)
    diagonal = jax.random.uniform(diag_key, (SUBDOMAIN_ROWS, SUBDOMAIN_COLS, MULTIPLIERS), jnp.float32, 0.6, 1.4)
    row_keys = jax.random.split(noise_key, SUBDOMAIN_ROWS)
    spread = 0.25 / jnp.sqrt(jnp.float32(2 * MULTIPLIERS))
    identity = jnp.eye(MULTIPLIERS, dtype=jnp.float32)

    def one_row(row_inputs):
        row_key, row_diagonal = row_inputs
        random_part = clipped_noise(row_key, (SUBDOMAIN_COLS, MULTIPLIERS, MULTIPLIERS))
        symmetric = (random_part + jnp.swapaxes(random_part, 1, 2)) * spread
        return (symmetric + row_diagonal[:, :, None] * identity).astype(jnp.bfloat16)
    return lax.map(one_row, (row_keys, diagonal))


def draw_dual_operator(key, part):
    return dense_operator(key, 31)


def draw_dirichlet(key, part):
    return dense_operator(key, 32)


def draw_coarse_inverse(key, part):
    salted = jax.random.fold_in(key, 33)
    diag_key, noise_key = jax.random.split(salted)
    diagonal = jax.random.uniform(diag_key, (COARSE_SIZE,), jnp.float32, 0.6, 1.4)
    random_part = clipped_noise(noise_key, (COARSE_SIZE, COARSE_SIZE))
    spread = 0.25 / jnp.sqrt(jnp.float32(2 * COARSE_SIZE))
    symmetric = (random_part + random_part.T) * spread + jnp.diag(diagonal)
    shaped = symmetric.reshape(SUBDOMAIN_ROWS, SUBDOMAIN_COLS, COARSE_MODES, SUBDOMAIN_ROWS, SUBDOMAIN_COLS, COARSE_MODES)
    return jnp.transpose(shaped, (0, 1, 2, 4, 3, 5)).reshape(SUBDOMAIN_ROWS, SUBDOMAIN_COLS * COARSE_MODES, SUBDOMAIN_COLS, SUBDOMAIN_ROWS * COARSE_MODES)


def interface_layout(key):
    salted = jax.random.fold_in(key, 41)
    keys_all = jax.random.split(salted, 6)
    grid_shape = (SUBDOMAIN_ROWS, SUBDOMAIN_COLS)
    lowest = FACE_SLOTS // 2
    count_x = jax.random.randint(keys_all[0], grid_shape, lowest, FACE_SLOTS + 1)
    count_y = jax.random.randint(keys_all[1], grid_shape, lowest, FACE_SLOTS + 1)
    row_index = lax.broadcasted_iota(jnp.int32, grid_shape, 0)
    col_index = lax.broadcasted_iota(jnp.int32, grid_shape, 1)
    full_row = jax.random.randint(keys_all[2], (), 0, SUBDOMAIN_ROWS - 1)
    full_col = jax.random.randint(keys_all[3], (), 0, SUBDOMAIN_COLS)
    count_x = jnp.where((row_index == full_row) & (col_index == full_col), FACE_SLOTS, count_x)
    count_x = jnp.where(row_index < SUBDOMAIN_ROWS - 1, count_x, 0).astype(jnp.int32)
    count_y = jnp.where(col_index < SUBDOMAIN_COLS - 1, count_y, 0).astype(jnp.int32)
    slot_index = lax.broadcasted_iota(jnp.int32, grid_shape + (FACE_SLOTS,), 2)

    def orders(order_key, live_counts):
        random_ranks = jax.random.randint(order_key, grid_shape + (FACE_SLOTS,), 0, 1 << 20)
        dead_flag = (slot_index >= live_counts[:, :, None]).astype(jnp.int32)
        scores = random_ranks * FACE_SLOTS + slot_index + dead_flag * ((1 << 20) * FACE_SLOTS)
        forward = jnp.argsort(scores, axis=2).astype(jnp.int32)
        backward = jnp.argsort(forward, axis=2).astype(jnp.int32)
        return (forward, backward)
    forward_x, backward_x = orders(keys_all[4], count_x)
    forward_y, backward_y = orders(keys_all[5], count_y)
    zero_row = jnp.zeros((1, SUBDOMAIN_COLS), jnp.int32)
    zero_col = jnp.zeros((SUBDOMAIN_ROWS, 1), jnp.int32)
    west_count = jnp.concatenate([zero_row, count_x[:-1]], axis=0)
    south_count = jnp.concatenate([zero_col, count_y[:, :-1]], axis=1)
    counts = jnp.stack([west_count, count_x, south_count, count_y], axis=2).astype(jnp.int32)
    west_lists = jnp.concatenate([slot_index[:1], backward_x[:-1]], axis=0)
    south_lists = jnp.concatenate([slot_index[:, :1], backward_y[:, :-1]], axis=1)
    partner_lists = jnp.stack([west_lists, forward_x, south_lists, forward_y], axis=2).astype(jnp.int32)
    return (counts, partner_lists)


def draw_face_counts(key, part):
    counts, partner_lists = interface_layout(key)
    return counts


def draw_partners(key, part):
    counts, partner_lists = interface_layout(key)
    return partner_lists


def setup_inputs(seed: int = 0) -> dict:
    arg_keys = jax.random.split(jax.random.key(seed), 8)
    load = draw_load(jax.random.fold_in(arg_keys[7], 71), 0)
    dual_operator = draw_dual_operator(jax.random.fold_in(arg_keys[7], 71), 0)
    dirichlet = draw_dirichlet(jax.random.fold_in(arg_keys[7], 71), 0)
    modes = draw_modes(jax.random.fold_in(arg_keys[7], 71), 0)
    coarse_inverse = draw_coarse_inverse(jax.random.fold_in(arg_keys[7], 71), 0)
    face_counts = draw_face_counts(jax.random.fold_in(arg_keys[7], 71), 0)
    partners = draw_partners(jax.random.fold_in(arg_keys[7], 71), 0)
    return {"load": load, "dual_operator": dual_operator, "dirichlet": dirichlet, "modes": modes, "coarse_inverse": coarse_inverse, "face_counts": face_counts, "partners": partners}


precise = lax.Precision.HIGHEST
spectrum_low = 0.5
spectrum_high = 4.0


def chebyshev_coefficients(iteration_count):
    center = (spectrum_high + spectrum_low) / 2.0
    radius = (spectrum_high - spectrum_low) / 2.0
    center_ratio = center / radius
    factor_prev = 1.0 / center_ratio
    result = [(1.0 / center, 0.0)]
    for iteration in range(1, iteration_count):
        factor = 1.0 / (2.0 * center_ratio - factor_prev)
        result.append((2.0 * factor / radius, factor * factor_prev))
        factor_prev = factor
    return result


def live_mask(face_counts):
    positions = lax.broadcasted_iota(jnp.int32, (1, 1, 4, FACE_SLOTS), 3)
    live_slots = (positions < face_counts[:, :, :, None]).astype(jnp.float32)
    return live_slots.reshape(SUBDOMAIN_ROWS, SUBDOMAIN_COLS, 1, MULTIPLIERS)


def interface_sum(values, partners, live_slots):
    face_blocks = values.reshape(SUBDOMAIN_ROWS, SUBDOMAIN_COLS, LOAD_COLUMNS, 4, FACE_SLOTS)
    face_west = face_blocks[:, :, :, 0]
    face_east = face_blocks[:, :, :, 1]
    face_south = face_blocks[:, :, :, 2]
    face_north = face_blocks[:, :, :, 3]
    empty_row = jnp.zeros_like(face_west[:1])
    empty_col = jnp.zeros_like(face_west[:, :1])
    from_west = jnp.concatenate([empty_row, face_east[:-1]], axis=0)
    from_east = jnp.concatenate([face_west[1:], empty_row], axis=0)
    from_south = jnp.concatenate([empty_col, face_north[:, :-1]], axis=1)
    from_north = jnp.concatenate([face_south[:, 1:], empty_col], axis=1)
    incoming = jnp.stack([from_west, from_east, from_south, from_north], axis=3)
    gather_index = jnp.broadcast_to(partners[:, :, None], incoming.shape).astype(jnp.int32)
    matched = jnp.take_along_axis(incoming, gather_index, axis=4)
    return (values + matched.reshape(values.shape)) * live_slots


def coarse_solve(vector, mode_rows, inverse_full):
    coeffs = jnp.einsum("abrm,abkm->abrk", vector, mode_rows, precision=precise)
    flat_coeffs = jnp.transpose(coeffs, (0, 1, 3, 2)).reshape(COARSE_SIZE, LOAD_COLUMNS)
    solved = jnp.dot(inverse_full, flat_coeffs, precision=precise, preferred_element_type=jnp.float32)
    solved = jnp.transpose(solved.reshape(SUBDOMAIN_ROWS, SUBDOMAIN_COLS, COARSE_MODES, LOAD_COLUMNS), (0, 1, 3, 2))
    return jnp.einsum("abrk,abkm->abrm", solved, mode_rows, precision=precise)


def local_products(vector, matrices):
    def one_row(row_inputs):
        row_vectors, row_matrices = row_inputs
        rounded = row_vectors.astype(jnp.bfloat16)
        rounded = lax.optimization_barrier(rounded)
        widened = rounded.astype(jnp.float32)
        return jnp.einsum("brm,bmn->brn", widened, row_matrices.astype(jnp.float32))
    return lax.map(one_row, (vector, matrices))


def reference(load, dual_operator, dirichlet, modes, coarse_inverse, face_counts, partners):
    live_slots = live_mask(face_counts)
    mode_rows = modes.astype(jnp.float32)
    inverse_full = jnp.transpose(
        coarse_inverse.reshape(SUBDOMAIN_ROWS, SUBDOMAIN_COLS, COARSE_MODES, SUBDOMAIN_COLS, SUBDOMAIN_ROWS, COARSE_MODES),
        (0, 1, 2, 4, 3, 5)).reshape(COARSE_SIZE, COARSE_SIZE)

    def assemble(values):
        return interface_sum(values, partners, live_slots)

    def project(vector):
        return vector - assemble(coarse_solve(vector, mode_rows, inverse_full))

    gap_values = assemble(load)
    residual = project(gap_values)
    multipliers = jnp.zeros_like(load)
    direction = jnp.zeros_like(load)
    for alpha_step, beta_step in chebyshev_coefficients(ITERATIONS):
        preconditioned = project(assemble(local_products(residual, dirichlet)))
        direction = alpha_step * preconditioned + beta_step * direction
        multipliers = multipliers + direction
        residual = residual - project(assemble(local_products(direction, dual_operator)))
    return multipliers, residual
```

```python
import functools

import jax
import jax.numpy as jnp
from jax import lax
from jax.experimental import pallas as pl
from jax.experimental.pallas import tpu as pltpu
from jax.sharding import PartitionSpec as P

f32 = jnp.float32
bf16 = jnp.bfloat16
precise = lax.Precision.HIGHEST
spectrum_low = 0.5
spectrum_high = 4.0

EVEN_FACES = (1, 0, 3, 2)
ODD_FACES = (0, 1, 2, 3)
ARRIVES = (0, 1, 3, 2)
REORDERED = (0, 2)


def round_up(value, unit):
    return -(-value // unit) * unit


def exchanges(rows, cols):
    def pairs(target):
        return [
            (a * cols + b, target(a, b)[0] * cols + target(a, b)[1])
            for a in range(rows)
            for b in range(cols)
        ]

    def along(a, b, step):
        return (a, b + step) if 0 <= b + step < cols else (a ^ 1, b)

    return (
        pairs(lambda a, b: (a ^ 1, b)),
        pairs(lambda a, b: ((a + 1 if a % 2 else a - 1) % rows, b)),
        pairs(lambda a, b: along(a, b, -1 if a % 2 else 1)),
        pairs(lambda a, b: along(a, b, 1 if a % 2 else -1)),
    )


def exchange(values, lists):
    return [lax.ppermute(value, ("gx", "gy"), pairs) for value, pairs in zip(values, lists)]


def chebyshev_coefficients():
    center = (spectrum_high + spectrum_low) / 2.0
    radius = (spectrum_high - spectrum_low) / 2.0
    center_ratio = center / radius
    factor_prev = 1.0 / center_ratio
    result = [(1.0 / center, 0.0)]
    factor = 1.0 / (2.0 * center_ratio - factor_prev)
    result.append((2.0 * factor / radius, factor * factor_prev))
    return result


def split3(value):
    high = value.astype(bf16)
    rest = value - high.astype(f32)
    middle = rest.astype(bf16)
    low = (rest - middle.astype(f32)).astype(bf16)
    return high, middle, low


def contract(left, right, left_dim, right_dim, precision=None):
    return lax.dot_general(
        left,
        right,
        (((left_dim,), (right_dim,)), ((), ())),
        precision=precision,
        preferred_element_type=f32,
    )


def by_parity(parity, even, odd):
    return jnp.where(parity == 0, even, odd)


def face_columns(value, slot, parity, width):
    even, odd = EVEN_FACES[slot], ODD_FACES[slot]
    return by_parity(
        parity,
        value[:, even * width : (even + 1) * width],
        value[:, odd * width : (odd + 1) * width],
    )


def reorder_matrix(partners, slot, parity, width, padded):
    plain = lax.broadcasted_iota(jnp.int32, (1, width), 1)

    def places(face):
        return partners[face : face + 1, :] if face in REORDERED else plain

    place = by_parity(parity, places(EVEN_FACES[slot]), places(ODD_FACES[slot]))
    rows = lax.broadcasted_iota(jnp.int32, (padded, width), 0)
    return jnp.where(rows == place, 1.0, 0.0).astype(bf16)


def reorder_exact(value, matrix, dim):
    count = value.shape[0]
    parts = contract(jnp.concatenate(split3(value), axis=0), matrix, 1, dim)
    return parts[:count] + (parts[count : 2 * count] + parts[2 * count :])


def live_columns(counts_ref, slot, parity, padded):
    count = by_parity(parity, counts_ref[EVEN_FACES[slot]], counts_ref[ODD_FACES[slot]])
    return lax.broadcasted_iota(jnp.int32, (1, padded), 1) < count


def load_kernel(parity_ref, load_ref, modes_ref, partners_ref, *face_refs):
    parity = parity_ref[0]
    width = partners_ref.shape[1]
    columns, count = load_ref.shape[0], modes_ref.shape[0]
    padded = face_refs[0].shape[1]
    for slot, face_ref in enumerate(face_refs):
        matrix = reorder_matrix(partners_ref[...], slot, parity, width, padded)
        values = face_columns(load_ref[...], slot, parity, width)
        modes = face_columns(modes_ref[...], slot, parity, width)
        face_ref[columns:, :] = jnp.zeros((face_ref.shape[0] - columns, padded), f32)
        face_ref[:columns, :] = reorder_exact(values, matrix, 1)
        face_ref[columns : columns + count, :] = contract(modes, matrix, 1, 1)


def matrix_kernel(parity_ref, matrix_ref, partners_ref, out_ref):
    parity = parity_ref[0]
    width = partners_ref.shape[1]
    padded = out_ref.shape[1] // 4
    reorder = [reorder_matrix(partners_ref[...], s, parity, width, padded) for s in range(4)]
    for slot in range(4):
        block = face_columns(matrix_ref[...], slot, parity, width)
        block = contract(block, reorder[slot], 1, 1).astype(bf16)
        for row_slot in range(4):
            even, odd = EVEN_FACES[row_slot], ODD_FACES[row_slot]
            rows = by_parity(
                parity,
                block[even * width : (even + 1) * width],
                block[odd * width : (odd + 1) * width],
            )
            out_ref[
                row_slot * padded : (row_slot + 1) * padded, slot * padded : (slot + 1) * padded
            ] = contract(reorder[row_slot], rows, 1, 0).astype(bf16)


def inverse_kernel(group, own_ref, *refs):
    neighbour_refs, (out_ref, rows_ref) = refs[:4], refs[4:]
    cols, count, length = own_ref.shape
    rows = length // count
    long, short = pack_counts(count)
    ratio = long // short
    rows_ref[...] = jnp.zeros(rows_ref.shape, f32)
    wide = rows * long
    source = lax.broadcasted_iota(jnp.int32, (length, wide), 0)
    target = lax.broadcasted_iota(jnp.int32, (length, wide), 1)
    source_row, source_mode = lax.div(source, count), lax.rem(source, count)
    target_row, target_place = lax.div(target, long), lax.rem(target, long)
    same = source_row == target_row
    places = [jnp.where(same & (source_mode == target_place), 1.0, 0.0).astype(f32)]
    for part in range(ratio):
        wanted = target_place - part * short
        inside = (wanted >= 0) & (wanted < short)
        places.append(
            jnp.where(same & inside & (source_mode == long + wanted), 1.0, 0.0).astype(f32)
        )
    gathered = [[] for _ in places]
    for e in range(cols):
        for index, ref in enumerate((own_ref, *neighbour_refs)):
            rows_ref[index * group : index * group + count, :] = ref[e]
        for part, place in enumerate(places):
            gathered[part].append(contract(rows_ref[...], place, 1, 0, precise))
    height = rows_ref.shape[0]
    for part, pieces in enumerate(gathered):
        out_ref[part * height : (part + 1) * height, :] = jnp.concatenate(pieces, axis=1)


def pack_counts(count):
    long = count * 3 // 4
    return long, count - long


def pack_coefficients(coeffs, count):
    long, short = pack_counts(count)
    pieces = long // short
    piece = coeffs.shape[1] // pieces
    tail = coeffs[long:count]
    side = jnp.concatenate([tail[:, i * piece : (i + 1) * piece] for i in range(pieces)], axis=0)
    return jnp.concatenate([coeffs[:long], side], axis=1)


def write_copies(out_ref, value):
    height = value.shape[0]
    copies = out_ref.shape[0] // height
    together = 8 if copies % 8 == 0 else 1
    block = jnp.concatenate([value] * together, axis=0)
    for i in range(copies // together):
        out_ref[i * together * height : (i + 1) * together * height, :] = block


def join_kernel(count, columns, first, parity_ref, counts_ref, *refs):
    sent, arrived = refs[:4], refs[4:8]
    parity = parity_ref[0]
    padded = sent[0].shape[1]
    if first:
        vector_ref, coeff_ref, modes_ref, extended_ref = refs[8:]
        group = modes_ref.shape[0]
        third = extended_ref.shape[0] // 3
        extended_ref[...] = jnp.zeros(extended_ref.shape, bf16)
    else:
        modes_ref, vector_ref, coeff_ref = refs[8:]
    for slot in range(4):
        live = live_columns(counts_ref, slot, parity, padded)
        place = slice(slot * padded, (slot + 1) * padded)
        own, other = sent[slot], arrived[ARRIVES.index(slot)]
        total = own[:columns, :] + other[:columns, :]
        vector_ref[:, place] = jnp.where(live, total, 0.0)
        if first:
            own_modes = jnp.where(live, own[columns : columns + group, :], 0.0).astype(bf16)
            other_modes = jnp.where(live, other[columns : columns + group, :], 0.0).astype(bf16)
            modes_ref[:, place] = own_modes
            for copy in range(3):
                base = copy * third
                extended_ref[base : base + group, place] = own_modes
                base += (1 + slot) * group
                extended_ref[base : base + group, place] = other_modes
    parts = contract(modes_ref[...], jnp.concatenate(split3(vector_ref[...]), axis=0), 1, 1)
    coeffs = parts[:, :columns] + (
        parts[:, columns : 2 * columns] + parts[:, 2 * columns : 3 * columns]
    )
    write_copies(coeff_ref, pack_coefficients(coeffs, count))


def projected(coeff_ref, inverse_ref, extended_ref, vector_ref):
    columns = vector_ref.shape[0]
    terms = contract(inverse_ref[...], coeff_ref[...], 1, 0, precise)
    height = extended_ref.shape[0] // 3
    solved = terms[:height, :columns] + jnp.concatenate(
        [
            terms[i * height : (i + 1) * height, columns:]
            for i in range(1, terms.shape[0] // height)
        ],
        axis=1,
    )
    parts = jnp.concatenate(split3(solved), axis=0)
    return vector_ref[...] - contract(parts, extended_ref[...], 0, 0)


def apply_matrix(vector, matrix_ref, face_refs):
    rounded = vector.astype(bf16)
    padded = matrix_ref.shape[1] // 4
    for slot, face_ref in enumerate(face_refs):
        face_ref[...] = contract(
            rounded, matrix_ref[:, slot * padded : (slot + 1) * padded], 1, 0
        )


def start_kernel(coeff_ref, inverse_ref, extended_ref, vector_ref, matrix_ref, *refs):
    residual_ref, face_refs = refs[0], refs[1:]
    residual = projected(coeff_ref, inverse_ref, extended_ref, vector_ref)
    residual_ref[...] = residual
    apply_matrix(residual, matrix_ref, face_refs)


def residual_kernel(coeff_ref, inverse_ref, extended_ref, vector_ref, matrix_ref, old_ref, *refs):
    residual_ref, face_refs = refs[0], refs[1:]
    residual = old_ref[...] - projected(coeff_ref, inverse_ref, extended_ref, vector_ref)
    residual_ref[...] = residual
    apply_matrix(residual, matrix_ref, face_refs)


def first_direction_kernel(alpha, coeff_ref, inverse_ref, extended_ref, vector_ref, matrix_ref, *refs):
    direction_ref, face_refs = refs[0], refs[1:]
    direction = alpha * projected(coeff_ref, inverse_ref, extended_ref, vector_ref)
    direction_ref[...] = direction
    apply_matrix(direction, matrix_ref, face_refs)


def direction_kernel(
    alpha, beta, coeff_ref, inverse_ref, extended_ref, vector_ref, matrix_ref, old_ref, *refs
):
    multipliers_ref, face_refs = refs[0], refs[1:]
    old = old_ref[...]
    preconditioned = projected(coeff_ref, inverse_ref, extended_ref, vector_ref)
    direction = alpha * preconditioned + beta * old
    multipliers_ref[...] = old + direction
    apply_matrix(direction, matrix_ref, face_refs)


def face_order(value, parity, partners, width):
    padded = value.shape[1] // 4
    slots = []
    for slot in range(4):
        matrix = reorder_matrix(partners, slot, parity, width, padded)
        slots.append(reorder_exact(value[:, slot * padded : (slot + 1) * padded], matrix, 0))
    return jnp.concatenate(
        [
            by_parity(parity, slots[EVEN_FACES.index(face)], slots[ODD_FACES.index(face)])
            for face in range(4)
        ],
        axis=1,
    )


def last_kernel(
    parity_ref, coeff_ref, inverse_ref, extended_ref, vector_ref, old_ref, partners_ref, out_ref
):
    residual = old_ref[...] - projected(coeff_ref, inverse_ref, extended_ref, vector_ref)
    out_ref[...] = face_order(residual, parity_ref[0], partners_ref[...], partners_ref.shape[1])


def multipliers_kernel(parity_ref, vector_ref, partners_ref, out_ref):
    out_ref[...] = face_order(
        vector_ref[...], parity_ref[0], partners_ref[...], partners_ref.shape[1]
    )


def call(kernel, outs, args, scalars=0, scratch=()):
    smem = pl.BlockSpec(memory_space=pltpu.SMEM)
    vmem = pl.BlockSpec(memory_space=pltpu.VMEM)
    size = sum(o.size * o.dtype.itemsize for o in (*outs, *args))
    return pl.pallas_call(
        kernel,
        out_shape=tuple(outs),
        in_specs=[smem] * scalars + [vmem] * (len(args) - scalars),
        out_specs=tuple([vmem] * len(outs)),
        scratch_shapes=list(scratch),
        compiler_params=pltpu.CompilerParams(
            vmem_limit_bytes=min(2 * size + (16 << 20), 56 << 20)
        ),
    )(*args)


def local(rows, cols, load, dual_operator, dirichlet, modes, coarse_inverse, face_counts, partners):
    devices = rows * cols
    columns, slots = load.shape[2:]
    width = partners.shape[3]
    padded = round_up(width, 128)
    count = modes.shape[2]
    group = round_up(count, 16)
    long, short = pack_counts(count)
    packed = columns + columns // (long // short)
    lists = exchanges(rows, cols)
    shape = jax.ShapeDtypeStruct
    vector = shape((columns, 4 * padded), f32)
    faces = [shape((columns, padded), f32)] * 4
    tall_faces = [shape((columns + group, padded), f32)] * 4
    matrix = shape((4 * padded, 4 * padded), bf16)
    coeff = shape((devices * long, packed), f32)
    height = 5 * group

    parity = (lax.axis_index("gx") % 2).astype(jnp.int32).reshape(1)
    counts = face_counts[0, 0]
    partners = partners[0, 0]
    chebyshev = chebyshev_coefficients()

    def everywhere(values):
        chunks = values.reshape(devices, long, 1, packed)
        return lax.all_to_all(chunks, ("gy", "gx"), 0, 0).reshape(devices * long, packed)

    sent = call(load_kernel, tall_faces, (parity, load[0, 0], modes[0, 0], partners), 1)
    arrived = exchange(sent, lists)
    own_rows = lax.all_to_all(
        coarse_inverse[0, :, 0, :].reshape(cols, count, rows * count), "gy", 0, 0
    )
    other_rows = exchange([own_rows] * 4, lists)
    (inverse,) = call(
        functools.partial(inverse_kernel, group),
        [shape(((1 + long // short) * height, devices * long), f32)],
        (own_rows, *[other_rows[ARRIVES.index(slot)] for slot in range(4)]),
        scratch=[pltpu.VMEM((height, rows * count), f32)],
    )
    (smoother,) = call(matrix_kernel, [matrix], (parity, dirichlet[0, 0], partners), 1)
    (operator,) = call(matrix_kernel, [matrix], (parity, dual_operator[0, 0], partners), 1)

    current, coeffs, mode_rows, extended = call(
        functools.partial(join_kernel, count, columns, True),
        [vector, coeff, shape((group, 4 * padded), bf16), shape((3 * height, 4 * padded), bf16)],
        (parity, counts, *sent, *arrived),
        2,
    )

    def join(sent):
        arrived = exchange(sent, lists)
        current, coeffs = call(
            functools.partial(join_kernel, count, columns, False),
            [vector, coeff],
            (parity, counts, *sent, *arrived, mode_rows),
            2,
        )
        return everywhere(coeffs), inverse, extended, current

    (alpha_0, _), (alpha_1, beta_1) = chebyshev
    residual, *sent = call(
        start_kernel,
        [vector, *faces],
        (everywhere(coeffs), inverse, extended, current, smoother),
    )
    direction, *sent = call(
        functools.partial(first_direction_kernel, alpha_0),
        [vector, *faces],
        (*join(sent), operator),
    )
    residual, *sent = call(
        residual_kernel, [vector, *faces], (*join(sent), smoother, residual)
    )
    multipliers, *sent = call(
        functools.partial(direction_kernel, alpha_1, beta_1),
        [vector, *faces],
        (*join(sent), operator, direction),
    )
    result = shape((columns, slots), f32)
    (residual,) = call(last_kernel, [result], (parity, *join(sent), residual, partners), 1)
    (multipliers,) = call(multipliers_kernel, [result], (parity, multipliers, partners), 1)
    return (multipliers[None, None], residual[None, None])


def solution(mesh):
    return jax.shard_map(
        functools.partial(local, mesh.shape["gx"], mesh.shape["gy"]),
        mesh=mesh,
        in_specs=(
            P("gx", "gy", None, None),
            P("gx", "gy", None, None),
            P("gx", "gy", None, None),
            P("gx", "gy", None, None),
            P("gx", None, "gy", None),
            P("gx", "gy", None),
            P("gx", "gy", None, None),
        ),
        out_specs=(P("gx", "gy", None, None), P("gx", "gy", None, None)),
        check_vma=False,
    )
```

```python
import functools

import jax
import jax.numpy as jnp
from jax import lax
from jax.experimental import pallas as pl
from jax.experimental.pallas import tpu as pltpu
from jax.sharding import PartitionSpec as P

f32 = jnp.float32
bf16 = jnp.bfloat16
precise = lax.Precision.HIGHEST
spectrum_low = 0.5
spectrum_high = 4.0

EVEN_FACES = (1, 0, 3, 2)
ODD_FACES = (0, 1, 2, 3)
ARRIVES = (0, 1, 3, 2)
REORDERED = (0, 2)


def round_up(value, unit):
    return -(-value // unit) * unit


def exchanges(rows, cols):
    def pairs(target):
        return [
            (a * cols + b, target(a, b)[0] * cols + target(a, b)[1])
            for a in range(rows)
            for b in range(cols)
        ]

    def along(a, b, step):
        return (a, b + step) if 0 <= b + step < cols else (a ^ 1, b)

    return (
        pairs(lambda a, b: (a ^ 1, b)),
        pairs(lambda a, b: ((a + 1 if a % 2 else a - 1) % rows, b)),
        pairs(lambda a, b: along(a, b, -1 if a % 2 else 1)),
        pairs(lambda a, b: along(a, b, 1 if a % 2 else -1)),
    )


def exchange(values, lists):
    return [lax.ppermute(value, ("gx", "gy"), pairs) for value, pairs in zip(values, lists)]


def chebyshev_coefficients():
    center = (spectrum_high + spectrum_low) / 2.0
    radius = (spectrum_high - spectrum_low) / 2.0
    center_ratio = center / radius
    factor_prev = 1.0 / center_ratio
    result = [(1.0 / center, 0.0)]
    factor = 1.0 / (2.0 * center_ratio - factor_prev)
    result.append((2.0 * factor / radius, factor * factor_prev))
    return result


def split3(value):
    high = value.astype(bf16)
    rest = value - high.astype(f32)
    middle = rest.astype(bf16)
    low = (rest - middle.astype(f32)).astype(bf16)
    return high, middle, low


def contract(left, right, left_dim, right_dim, precision=None):
    return lax.dot_general(
        left,
        right,
        (((left_dim,), (right_dim,)), ((), ())),
        precision=precision,
        preferred_element_type=f32,
    )


def by_parity(parity, even, odd):
    return jnp.where(parity == 0, even, odd)


def face_columns(value, slot, parity, width):
    even, odd = EVEN_FACES[slot], ODD_FACES[slot]
    return by_parity(
        parity,
        value[:, even * width : (even + 1) * width],
        value[:, odd * width : (odd + 1) * width],
    )


def reorder_matrix(partners, slot, parity, width, padded):
    plain = lax.broadcasted_iota(jnp.int32, (1, width), 1)

    def places(face):
        return partners[face : face + 1, :] if face in REORDERED else plain

    place = by_parity(parity, places(EVEN_FACES[slot]), places(ODD_FACES[slot]))
    rows = lax.broadcasted_iota(jnp.int32, (padded, width), 0)
    return jnp.where(rows == place, 1.0, 0.0).astype(bf16)


def reorder_exact(value, matrix, dim):
    count = value.shape[0]
    parts = contract(jnp.concatenate(split3(value), axis=0), matrix, 1, dim)
    return parts[:count] + (parts[count : 2 * count] + parts[2 * count :])


def row_parity():
    return lax.rem(lax.axis_index("gx"), 2)


def pack_counts(count):
    long = count * 3 // 4
    return long, count - long


def pack_coefficients(coeffs, count):
    long, short = pack_counts(count)
    pieces = long // short
    piece = coeffs.shape[1] // pieces
    tail = coeffs[long:count]
    side = jnp.concatenate([tail[:, i * piece : (i + 1) * piece] for i in range(pieces)], axis=0)
    return jnp.concatenate([coeffs[:long], side], axis=1)


def write_copies(out_ref, value):
    height = value.shape[0]
    copies = out_ref.shape[0] // height
    together = 8 if copies % 8 == 0 else 1
    block = jnp.concatenate([value] * together, axis=0)
    for i in range(copies // together):
        out_ref[i * together * height : (i + 1) * together * height, :] = block


def inverse_places(index, group, length, padded):
    block = round_up(length, 128)
    beside = max(padded // block, 1)
    below = -(-length // padded)
    return [
        (
            ((index // beside) * below + part) * group,
            (index % beside) * block,
            slice(part * padded, min(length, (part + 1) * padded)),
        )
        for part in range(below)
    ]


def inverse_lines(cols, group, length, padded):
    return max(
        place[0] + group
        for index in range(cols)
        for place in inverse_places(index, group, length, padded)
    )


def load_kernel(
    load_hbm, modes_hbm, partners_hbm, counts_hbm,
    face_0, face_1, face_2, face_3, live_ref, reorder_ref,
    load_ref, modes_ref, partners_ref, counts_ref, sems,
):
    copies = [
        pltpu.make_async_copy(source, target, sems.at[i])
        for i, (source, target) in enumerate(
            (
                (load_hbm.at[0, 0], load_ref),
                (modes_hbm.at[0, 0], modes_ref),
                (partners_hbm.at[0, 0], partners_ref),
                (counts_hbm.at[0], counts_ref),
            )
        )
    ]
    for copy in copies:
        copy.start()
    for copy in copies:
        copy.wait()
    parity = row_parity()
    width = partners_ref.shape[1]
    columns, count = load_ref.shape[0], modes_ref.shape[0]
    padded = face_0.shape[1]
    for slot, face_ref in enumerate((face_0, face_1, face_2, face_3)):
        matrix = reorder_matrix(partners_ref[...], slot, parity, width, padded)
        reorder_ref[slot] = matrix
        values = face_columns(load_ref[...], slot, parity, width)
        modes = face_columns(modes_ref[...], slot, parity, width)
        face_ref[columns:, :] = jnp.zeros((face_ref.shape[0] - columns, padded), f32)
        face_ref[:columns, :] = reorder_exact(values, matrix, 1)
        face_ref[columns : columns + count, :] = contract(modes, matrix, 1, 1)
        live = by_parity(
            parity, counts_ref[0, EVEN_FACES[slot]], counts_ref[0, ODD_FACES[slot]]
        )
        places = lax.broadcasted_iota(jnp.int32, (live_ref.shape[0], padded), 1)
        live_ref[:, slot * padded : (slot + 1) * padded] = jnp.where(places < live, 1.0, 0.0)


def matrix_kernel(matrix_hbm, reorder_ref, after_hbm, out_ref, matrix_ref, sems):
    width = matrix_ref.shape[0] // 4
    copies = [
        pltpu.make_async_copy(
            matrix_hbm.at[0, 0, pl.ds(face * width, width)],
            matrix_ref.at[pl.ds(face * width, width)],
            sems.at[face],
        )
        for face in range(4)
    ]
    for copy in copies:
        copy.start()
    parity = row_parity()
    padded = out_ref.shape[1] // 4
    for face, copy in enumerate(copies):
        copy.wait()
        rows = matrix_ref[face * width : (face + 1) * width, :]
        row_slot = by_parity(parity, EVEN_FACES.index(face), ODD_FACES.index(face))
        place = pl.ds(pl.multiple_of(row_slot * padded, padded), padded)
        for slot in range(4):
            block = face_columns(rows, slot, parity, width)
            block = contract(block, reorder_ref[slot], 1, 1).astype(bf16)
            out_ref[place, slot * padded : (slot + 1) * padded] = contract(
                reorder_ref[row_slot], block, 1, 0
            ).astype(bf16)


def rows_kernel(count, base, *refs):
    part_refs, (first_ref, second_ref, rows_ref) = refs[2:-3], refs[-3:]
    cols, here = len(part_refs), lax.axis_index("gy")
    group, length = rows_ref.shape[1:]
    rows_ref[...] = jnp.zeros(rows_ref.shape, f32)
    for step, part_ref in enumerate(part_refs):
        source = lax.rem(here + cols - step, cols)
        rows_ref[source, :count, :] = part_ref[0, pl.ds(here * count, count), 0, :]
    for face_ref in (first_ref, second_ref):
        for e in range(cols):
            for line, lane, part in inverse_places(e, group, length, face_ref.shape[1]):
                face_ref[
                    base + line : base + line + group, lane : lane + part.stop - part.start
                ] = rows_ref[e, :, part]


def inverse_kernel(count, base, *refs):
    face_refs = refs[:3]
    part_refs, (out_ref, rows_ref) = refs[3:-3], refs[-2:]
    cols = len(part_refs)
    parity, here = row_parity(), lax.axis_index("gy")
    north, south = jnp.minimum(here + 1, cols - 1), jnp.maximum(here - 1, 0)
    length = rows_ref.shape[2]
    group = round_up(count, 8)
    rows, height = length // count, rows_ref.shape[1]
    long, short = pack_counts(count)
    rows_ref[...] = jnp.zeros(rows_ref.shape, f32)
    for e in range(cols):
        for i, ref in enumerate(face_refs):
            for line, lane, part in inverse_places(e, group, length, ref.shape[1]):
                rows_ref[e, i * count : (i + 1) * count, part] = ref[
                    base + line : base + line + count, lane : lane + part.stop - part.start
                ]
    for step, part_ref in enumerate(part_refs):
        source_col = lax.rem(here + cols - step, cols)
        for i, row in ((3, jnp.where(parity == 0, north, south)), (4, jnp.where(parity == 0, south, north))):
            rows_ref[source_col, i * count : (i + 1) * count, :] = part_ref[
                0, pl.ds(row * count, count), 0, :
            ]
    wide = rows * long
    source = lax.broadcasted_iota(jnp.int32, (length, wide), 0)
    target = lax.broadcasted_iota(jnp.int32, (length, wide), 1)
    source_row, source_mode = lax.div(source, count), lax.rem(source, count)
    target_row, target_place = lax.div(target, long), lax.rem(target, long)
    same = source_row == target_row
    places = [jnp.where(same & (source_mode == target_place), 1.0, 0.0).astype(bf16)]
    for part in range(long // short):
        wanted = target_place - part * short
        inside = (wanted >= 0) & (wanted < short)
        places.append(
            jnp.where(same & inside & (source_mode == long + wanted), 1.0, 0.0).astype(bf16)
        )
    everything = cols * wide
    gathered = [[] for _ in places]
    for e in range(cols):
        high, middle, _ = split3(rows_ref[e])
        halves = jnp.concatenate([high, middle], axis=0)
        for part, place in enumerate(places):
            gathered[part].append(contract(halves, place, 1, 0))
    for part, pieces in enumerate(gathered):
        both = jnp.concatenate(pieces, axis=1).astype(bf16)
        place = slice(part * height, (part + 1) * height)
        out_ref[place, :] = jnp.concatenate([both[:height], both[:height], both[height:]], axis=1)


def coefficients(vector, columns_ref, count):
    high, middle, _ = split3(vector)
    terms = jnp.dot(
        jnp.concatenate([high, middle], axis=0), columns_ref[...], preferred_element_type=f32
    )
    columns = vector.shape[0]
    coeffs = (terms[:columns] + terms[columns:]).T
    return pack_coefficients(coeffs, count)


def join_faces(sent, arrived, live_ref, vector_ref):
    columns, padded = vector_ref.shape[0], sent[0].shape[1]
    for slot in range(4):
        place = slice(slot * padded, (slot + 1) * padded)
        own, other = sent[slot], arrived[ARRIVES.index(slot)]
        total = own[:columns, :] + other[:columns, :]
        vector_ref[:, place] = jnp.where(live_ref[:1, place] > 0.0, total, 0.0)


def first_join_kernel(count, *refs):
    sent, arrived, live_ref = refs[:4], refs[4:8], refs[8]
    vector_ref, coeff_ref, columns_ref, extended_ref, rows_ref = refs[-5:]
    columns, padded = vector_ref.shape[0], sent[0].shape[1]
    group = sent[3].shape[0] - columns
    half = rows_ref.shape[0]
    join_faces(sent, arrived, live_ref, vector_ref)
    rows_ref[...] = jnp.zeros(rows_ref.shape, f32)
    blank = jnp.zeros((columns_ref.shape[1] - group, padded), f32)
    for slot in range(4):
        place = slice(slot * padded, (slot + 1) * padded)
        live = live_ref[:1, place]
        own = sent[slot][columns : columns + group, :] * live
        other = arrived[ARRIVES.index(slot)][columns : columns + group, :] * live
        columns_ref[place, :] = jnp.concatenate([own, blank], axis=0).T.astype(bf16)
        rows_ref[:count, place] = own[:count]
        rows_ref[(1 + slot) * count : (2 + slot) * count, place] = other[:count]
    extended = rows_ref[...].astype(bf16)
    extended_ref[:half, :] = extended
    extended_ref[half:, :] = extended
    write_copies(coeff_ref, coefficients(vector_ref[...], columns_ref, count))


def join_kernel(count, *refs):
    sent, arrived, live_ref, columns_ref = refs[:4], refs[4:8], refs[8], refs[9]
    vector_ref, coeff_ref = refs[-2:]
    join_faces(sent, arrived, live_ref, vector_ref)
    write_copies(coeff_ref, coefficients(vector_ref[...], columns_ref, count))


def projected(coeff_ref, inverse_ref, extended_ref, vector_ref):
    columns, height = vector_ref.shape[0], extended_ref.shape[0] // 2
    high, middle, _ = split3(coeff_ref[...])
    terms = contract(inverse_ref[...], jnp.concatenate([high, middle, high], axis=0), 1, 0)
    solved = terms[:height, :columns] + jnp.concatenate(
        [
            terms[i * height : (i + 1) * height, columns:]
            for i in range(1, terms.shape[0] // height)
        ],
        axis=1,
    )
    high, middle, _ = split3(solved)
    parts = jnp.concatenate([high, middle], axis=0)
    return vector_ref[...] - contract(parts, extended_ref[...], 0, 0)


def apply_matrix(vector, matrix_ref, face_refs):
    rounded = vector.astype(bf16)
    padded = matrix_ref.shape[1] // 4
    for slot, face_ref in enumerate(face_refs):
        face_ref[...] = contract(
            rounded, matrix_ref[:, slot * padded : (slot + 1) * padded], 1, 0
        )


def start_kernel(coeff_ref, inverse_ref, extended_ref, vector_ref, matrix_ref, *refs):
    residual_ref, face_refs = refs[0], refs[1:]
    residual = projected(coeff_ref, inverse_ref, extended_ref, vector_ref)
    residual_ref[...] = residual
    apply_matrix(residual, matrix_ref, face_refs)


def residual_kernel(coeff_ref, inverse_ref, extended_ref, vector_ref, matrix_ref, old_ref, *refs):
    residual_ref, face_refs = refs[0], refs[1:]
    residual = old_ref[...] - projected(coeff_ref, inverse_ref, extended_ref, vector_ref)
    residual_ref[...] = residual
    apply_matrix(residual, matrix_ref, face_refs)


def first_direction_kernel(alpha, coeff_ref, inverse_ref, extended_ref, vector_ref, matrix_ref, *refs):
    direction_ref, face_refs = refs[0], refs[1:]
    direction = alpha * projected(coeff_ref, inverse_ref, extended_ref, vector_ref)
    direction_ref[...] = direction
    apply_matrix(direction, matrix_ref, face_refs)


def direction_kernel(
    alpha, beta, coeff_ref, inverse_ref, extended_ref, vector_ref, matrix_ref, old_ref, *refs
):
    multipliers_ref, face_refs = refs[0], refs[1:]
    old = old_ref[...]
    preconditioned = projected(coeff_ref, inverse_ref, extended_ref, vector_ref)
    direction = alpha * preconditioned + beta * old
    multipliers_ref[...] = old + direction
    apply_matrix(direction, matrix_ref, face_refs)


def face_order(value, reorder_ref):
    parity = row_parity()
    padded = value.shape[1] // 4
    slots = [
        reorder_exact(value[:, slot * padded : (slot + 1) * padded], reorder_ref[slot], 0)
        for slot in range(4)
    ]
    return jnp.concatenate(
        [
            by_parity(parity, slots[EVEN_FACES.index(face)], slots[ODD_FACES.index(face)])
            for face in range(4)
        ],
        axis=1,
    )


def last_kernel(coeff_ref, inverse_ref, extended_ref, vector_ref, old_ref, reorder_ref, out_ref):
    residual = old_ref[...] - projected(coeff_ref, inverse_ref, extended_ref, vector_ref)
    out_ref[...] = face_order(residual, reorder_ref)


def multipliers_kernel(vector_ref, reorder_ref, out_ref):
    out_ref[...] = face_order(vector_ref[...], reorder_ref)


def call(kernel, outs, args, hbm=(), after=(), scratch=(), aliases={}):
    vmem = pl.BlockSpec(memory_space=pltpu.VMEM)
    outside = pl.BlockSpec(memory_space=pltpu.HBM)
    anywhere = pl.BlockSpec(memory_space=pl.ANY)
    size = sum(o.size * o.dtype.itemsize for o in (*outs, *args))
    args = [
        pltpu.with_memory_space_constraint(arg, pltpu.HBM) if i in hbm else arg
        for i, arg in enumerate(args)
    ]
    return pl.pallas_call(
        kernel,
        out_shape=tuple(outs),
        in_specs=[
            outside if i in hbm else anywhere if i in after else vmem for i in range(len(args))
        ],
        out_specs=tuple([vmem] * len(outs)),
        scratch_shapes=list(scratch),
        input_output_aliases=aliases,
        compiler_params=pltpu.CompilerParams(vmem_limit_bytes=min(size + (8 << 20), 56 << 20)),
    )(*args)


def local(rows, cols, load, dual_operator, dirichlet, modes, coarse_inverse, face_counts, partners):
    devices = rows * cols
    columns, slots = load.shape[2:]
    width = partners.shape[3]
    padded = round_up(width, 128)
    count = modes.shape[2]
    group = round_up(count, 8)
    height = round_up(5 * count, 16)
    long, short = pack_counts(count)
    packed = columns + columns // (long // short)
    lists = exchanges(rows, cols)
    shape = jax.ShapeDtypeStruct
    vector = shape((columns, 4 * padded), f32)
    faces = [shape((columns, padded), f32)] * 4
    base = columns + group
    lines = inverse_lines(cols, group, rows * count, padded)
    tall_faces = [shape((base + extra, padded), f32) for extra in (lines, lines, 0, 0)]
    matrix = shape((4 * padded, 4 * padded), bf16)
    coeff = shape((devices * long, packed), f32)
    result = shape((columns, slots), f32)
    (alpha_0, _), (alpha_1, beta_1) = chebyshev_coefficients()

    def everywhere(values):
        chunks = values.reshape(devices, long, 1, packed)
        return lax.all_to_all(chunks, ("gy", "gx"), 0, 0).reshape(devices * long, packed)

    def reordered(values, after):
        return call(
            matrix_kernel,
            [matrix],
            (values, reorder, after),
            (0,),
            (2,),
            [pltpu.VMEM((slots, slots), bf16), pltpu.SemaphoreType.DMA((4,))],
        )[0]

    parts = [coarse_inverse] + [
        lax.ppermute(coarse_inverse, "gy", [(b, (b + step) % cols) for b in range(cols)])
        for step in range(1, cols)
    ]
    *sent, live, reorder = call(
        load_kernel,
        [
            *tall_faces,
            shape((8, 4 * padded), f32),
            shape((4, padded, width), bf16),
        ],
        (load, modes, partners, face_counts),
        (0, 1, 2, 3),
        (),
        [
            pltpu.VMEM((columns, slots), f32),
            pltpu.VMEM((count, slots), bf16),
            pltpu.VMEM((4, width), jnp.int32),
            pltpu.SMEM((1, 4), jnp.int32),
            pltpu.SemaphoreType.DMA((4,)),
        ],
    )
    sent[:2] = call(
        functools.partial(rows_kernel, count, base),
        tall_faces[:2],
        (*sent[:2], *parts),
        scratch=[pltpu.VMEM((cols, group, rows * count), f32)],
        aliases={0: 0, 1: 1},
    )
    arrived = exchange(sent, lists)
    smoother = reordered(dirichlet, sent[0])
    (inverse,) = call(
        functools.partial(inverse_kernel, count, base),
        [shape(((1 + long // short) * height, 3 * devices * long), bf16)],
        (sent[0], *arrived[:2], *parts, smoother),
        (),
        (3 + cols,),
        [pltpu.VMEM((cols, height, rows * count), f32)],
    )
    current, coeffs, mode_columns, extended = call(
        functools.partial(first_join_kernel, count),
        [vector, coeff, shape((4 * padded, 128), bf16), shape((2 * height, 4 * padded), bf16)],
        (*sent, *arrived, live, inverse),
        (),
        (9,),
        [pltpu.VMEM((height, 4 * padded), f32)],
    )

    def join(sent, *before, last=False):
        arrived = exchange(sent, lists)
        current, coeffs = call(
            functools.partial(join_kernel, count),
            [vector, coeff],
            (*sent, *arrived, live, mode_columns, *before),
            (10,) if last else (),
            (10,),
        )
        return everywhere(coeffs), inverse, extended, current

    residual, *sent = call(
        start_kernel,
        [vector, *faces],
        (everywhere(coeffs), inverse, extended, current, smoother),
    )
    operator = reordered(dual_operator, sent[0])
    direction, *sent = call(
        functools.partial(first_direction_kernel, alpha_0),
        [vector, *faces],
        (*join(sent, operator), operator),
    )
    residual, *sent = call(
        residual_kernel, [vector, *faces], (*join(sent), smoother, residual)
    )
    multipliers, *sent = call(
        functools.partial(direction_kernel, alpha_1, beta_1),
        [vector, *faces],
        (*join(sent), operator, direction),
    )
    (multipliers,) = call(multipliers_kernel, [result], (multipliers, reorder))
    (residual,) = call(
        last_kernel, [result], (*join(sent, multipliers, last=True), residual, reorder)
    )
    return (multipliers[None, None], residual[None, None])


def solution(mesh):
    return jax.shard_map(
        functools.partial(local, mesh.shape["gx"], mesh.shape["gy"]),
        mesh=mesh,
        in_specs=(
            P("gx", "gy", None, None),
            P("gx", "gy", None, None),
            P("gx", "gy", None, None),
            P("gx", "gy", None, None),
            P("gx", None, "gy", None),
            P("gx", "gy", None),
            P("gx", "gy", None, None),
        ),
        out_specs=(P("gx", "gy", None, None), P("gx", "gy", None, None)),
        check_vma=False,
    )
```

```python
import functools

import jax
import jax.numpy as jnp
from jax import lax
from jax.experimental import pallas as pl
from jax.experimental.pallas import tpu as pltpu
from jax.sharding import PartitionSpec as P

f32 = jnp.float32
bf16 = jnp.bfloat16
precise = lax.Precision.HIGHEST
spectrum_low = 0.5
spectrum_high = 4.0

EVEN_FACES = (0, 3, 2, 1)
ODD_FACES = (1, 2, 3, 0)
ARRIVES = (0, 2, 1, 3)
REORDERED = (0, 2)


PRODUCTS = ((0, 0), (0, 1), (1, 0), (1, 1), (0, 2), (2, 0))


def round_up(value, unit):
    return -(-value // unit) * unit


def exchanges(rows, cols):
    def pairs(target):
        return [
            (a * cols + b, target(a, b)[0] * cols + target(a, b)[1])
            for a in range(rows)
            for b in range(cols)
        ]

    def along(a, b, step):
        return (a, b + step) if 0 <= b + step < cols else (a ^ 1, b)

    return (
        pairs(lambda a, b: ((a + 1 if a % 2 else a - 1) % rows, b)),
        pairs(lambda a, b: along(a, b, -1 if a % 2 else 1)),
        pairs(lambda a, b: along(a, b, 1 if a % 2 else -1)),
        pairs(lambda a, b: (a ^ 1, b)),
    )


def exchange(values, lists):
    return [lax.ppermute(value, ("gx", "gy"), pairs) for value, pairs in zip(values, lists)]


def chebyshev_coefficients():
    center = (spectrum_high + spectrum_low) / 2.0
    radius = (spectrum_high - spectrum_low) / 2.0
    center_ratio = center / radius
    factor_prev = 1.0 / center_ratio
    result = [(1.0 / center, 0.0)]
    factor = 1.0 / (2.0 * center_ratio - factor_prev)
    result.append((2.0 * factor / radius, factor * factor_prev))
    return result


def split3(value):
    high = value.astype(bf16)
    rest = value - high.astype(f32)
    middle = rest.astype(bf16)
    low = (rest - middle.astype(f32)).astype(bf16)
    return high, middle, low


def contract(left, right, left_dim, right_dim, precision=None):
    return lax.dot_general(
        left,
        right,
        (((left_dim,), (right_dim,)), ((), ())),
        precision=precision,
        preferred_element_type=f32,
    )


def by_parity(parity, even, odd):
    return jnp.where(parity == 0, even, odd)


def slot_of(face, parity):
    return by_parity(parity, EVEN_FACES.index(face), ODD_FACES.index(face))


def slots_from(faces, parity):
    return [by_parity(parity, faces[EVEN_FACES[j]], faces[ODD_FACES[j]]) for j in range(4)]


def reorder_matrix(place, padded):
    rows = lax.broadcasted_iota(jnp.int32, (padded, place.shape[1]), 0)
    return jnp.where(rows == place, 1.0, 0.0).astype(bf16)


def widened(value, padded):
    blank = jnp.zeros((value.shape[0], padded - value.shape[1]), value.dtype)
    return jnp.concatenate([value, blank], axis=1)


def reorder_exact(value, matrix, dim):
    count = value.shape[0]
    parts = contract(jnp.concatenate(split3(value), axis=0), matrix, 1, dim)
    return parts[:count] + (parts[count : 2 * count] + parts[2 * count :])


def row_parity():
    return lax.rem(lax.axis_index("gx"), 2)


def pack_counts(count):
    long = count * 3 // 4
    return long, count - long


def pack_coefficients(coeffs, count):
    long, short = pack_counts(count)
    pieces = long // short
    piece = coeffs.shape[1] // pieces
    tail = coeffs[long:count]
    side = jnp.concatenate([tail[:, i * piece : (i + 1) * piece] for i in range(pieces)], axis=0)
    return jnp.concatenate([coeffs[:long], side], axis=1)


def write_copies(out_ref, value):
    height = value.shape[0]
    copies = out_ref.shape[0] // height
    together = 8 if copies % 8 == 0 else 1
    block = jnp.concatenate([value] * together, axis=0)
    for i in range(copies // together):
        out_ref[i * together * height : (i + 1) * together * height, :] = block


def inverse_places(index, group, length, padded):
    block = round_up(length, 128)
    beside = max(padded // block, 1)
    below = -(-length // padded)
    return [
        (
            ((index // beside) * below + part) * group,
            (index % beside) * block,
            slice(part * padded, min(length, (part + 1) * padded)),
        )
        for part in range(below)
    ]


def inverse_lines(cols, group, length, padded):
    return max(
        place[0] + group
        for index in range(cols)
        for place in inverse_places(index, group, length, padded)
    )


def load_kernel(
    load_hbm, modes_hbm, partners_hbm, counts_hbm, matrix_hbm, inverse_hbm,
    slot_0, slot_1, slot_2, slot_3, live_ref, reorder_ref, matrix_ref, inverse_ref,
    load_ref, modes_ref, partners_ref, counts_ref, sems,
):
    copies = [
        pltpu.make_async_copy(source, target, sems.at[i])
        for i, (source, target) in enumerate(
            (
                (partners_hbm.at[0, 0], partners_ref),
                (load_hbm.at[0, 0], load_ref),
                (modes_hbm.at[0, 0], modes_ref),
                (counts_hbm.at[0], counts_ref),
                (inverse_hbm, inverse_ref),
                (matrix_hbm.at[0, 0], matrix_ref),
            )
        )
    ]
    for copy in copies:
        copy.start()
    for copy in copies[:4]:
        copy.wait()
    parity = row_parity()
    width = partners_ref.shape[1]
    columns, count = load_ref.shape[0], modes_ref.shape[0]
    padded = slot_0.shape[1]
    values, modes = [], []
    for face in range(4):
        place = slice(face * width, (face + 1) * width)
        if face in REORDERED:
            matrix = reorder_matrix(partners_ref[face : face + 1, :], padded)
            reorder_ref[REORDERED.index(face)] = matrix
            values.append(reorder_exact(load_ref[:, place], matrix, 1))
            modes.append(contract(modes_ref[:, place], matrix, 1, 1))
        else:
            values.append(widened(load_ref[:, place], padded))
            modes.append(widened(modes_ref[:, place], padded).astype(f32))
    values, modes = slots_from(values, parity), slots_from(modes, parity)
    for slot, slot_ref in enumerate((slot_0, slot_1, slot_2, slot_3)):
        slot_ref[columns:, :] = jnp.zeros((slot_ref.shape[0] - columns, padded), f32)
        slot_ref[:columns, :] = values[slot]
        slot_ref[columns : columns + count, :] = modes[slot]
        live = by_parity(
            parity, counts_ref[0, EVEN_FACES[slot]], counts_ref[0, ODD_FACES[slot]]
        )
        places = lax.broadcasted_iota(jnp.int32, (live_ref.shape[0], padded), 1)
        live_ref[:, slot * padded : (slot + 1) * padded] = jnp.where(places < live, 1.0, 0.0)
    for copy in copies[4:]:
        copy.wait()


def reorder_operator(matrix_ref, reorder_ref, out_ref, columns_ref):
    parity = row_parity()
    width, padded = matrix_ref.shape[1] // 4, out_ref.shape[1] // 4

    def slot_place(face):
        return pl.ds(pl.multiple_of(slot_of(face, parity) * padded, padded), padded)

    for face in range(4):
        block = matrix_ref[:, face * width : (face + 1) * width]
        if face in REORDERED:
            block = contract(block, reorder_ref[REORDERED.index(face)], 1, 1).astype(bf16)
        else:
            block = widened(block, padded)
        columns_ref[:, slot_place(face)] = block
    for face in range(4):
        block = columns_ref[face * width : (face + 1) * width, :]
        if face in REORDERED:
            block = contract(reorder_ref[REORDERED.index(face)], block, 1, 0).astype(bf16)
        else:
            blank = jnp.zeros((padded - width, block.shape[1]), bf16)
            block = jnp.concatenate([block, blank], axis=0)
        out_ref[slot_place(face), :] = block


def smoother_kernel(matrix_ref, reorder_ref, next_hbm, after_hbm, out_ref, next_ref, columns_ref, sem):
    copy = pltpu.make_async_copy(next_hbm.at[0, 0], next_ref, sem)
    copy.start()
    reorder_operator(matrix_ref, reorder_ref, out_ref, columns_ref)
    copy.wait()


def operator_kernel(matrix_ref, reorder_ref, after_hbm, out_ref, columns_ref):
    reorder_operator(matrix_ref, reorder_ref, out_ref, columns_ref)


def rows_kernel(count, base, *refs):
    part_refs, (first_ref, second_ref, rows_ref) = refs[2:-3], refs[-3:]
    cols, here = len(part_refs), lax.axis_index("gy")
    group, length = rows_ref.shape[1:]
    rows_ref[...] = jnp.zeros(rows_ref.shape, f32)
    for step, part_ref in enumerate(part_refs):
        source = lax.rem(here + cols - step, cols)
        rows_ref[source, :count, :] = part_ref[0, pl.ds(here * count, count), 0, :]
    for face_ref in (first_ref, second_ref):
        for e in range(cols):
            for line, lane, part in inverse_places(e, group, length, face_ref.shape[1]):
                face_ref[
                    base + line : base + line + group, lane : lane + part.stop - part.start
                ] = rows_ref[e, :, part]


def inverse_kernel(count, base, *refs):
    face_refs = refs[:3]
    part_refs, (out_ref, rows_ref) = refs[3:-3], refs[-2:]
    cols = len(part_refs)
    parity, here = row_parity(), lax.axis_index("gy")
    north, south = jnp.minimum(here + 1, cols - 1), jnp.maximum(here - 1, 0)
    length = rows_ref.shape[2]
    group = round_up(count, 8)
    rows, height = length // count, rows_ref.shape[1]
    long, short = pack_counts(count)
    rows_ref[...] = jnp.zeros(rows_ref.shape, f32)
    for e in range(cols):
        for i, ref in zip((0, 1, 4), face_refs):
            for line, lane, part in inverse_places(e, group, length, ref.shape[1]):
                rows_ref[e, i * count : (i + 1) * count, part] = ref[
                    base + line : base + line + count, lane : lane + part.stop - part.start
                ]
    for step, part_ref in enumerate(part_refs):
        source_col = lax.rem(here + cols - step, cols)
        for i, row in ((2, jnp.where(parity == 0, north, south)), (3, jnp.where(parity == 0, south, north))):
            rows_ref[source_col, i * count : (i + 1) * count, :] = part_ref[
                0, pl.ds(row * count, count), 0, :
            ]
    wide = rows * long
    source = lax.broadcasted_iota(jnp.int32, (length, wide), 0)
    target = lax.broadcasted_iota(jnp.int32, (length, wide), 1)
    source_row, source_mode = lax.div(source, count), lax.rem(source, count)
    target_row, target_place = lax.div(target, long), lax.rem(target, long)
    same = source_row == target_row
    places = [jnp.where(same & (source_mode == target_place), 1.0, 0.0).astype(bf16)]
    for part in range(long // short):
        wanted = target_place - part * short
        inside = (wanted >= 0) & (wanted < short)
        places.append(
            jnp.where(same & inside & (source_mode == long + wanted), 1.0, 0.0).astype(bf16)
        )
    place = jnp.concatenate(places, axis=1)
    gathered = [[] for _ in places]
    for e in range(cols):
        pieces = jnp.concatenate(split3(rows_ref[e]), axis=0)
        moved = contract(pieces, place, 1, 0)
        for part in range(len(places)):
            gathered[part].append(moved[:, part * wide : (part + 1) * wide])
    for part, pieces in enumerate(gathered):
        high, middle, low = (
            jnp.concatenate([p[k * height : (k + 1) * height] for p in pieces], axis=1)
            for k in range(3)
        )
        factors = [(high, middle, low)[k] for k, _ in PRODUCTS]
        out_ref[part * height : (part + 1) * height, :] = jnp.concatenate(factors, axis=1).astype(
            bf16
        )


def coefficients(vector, columns_ref, count):
    terms = jnp.dot(
        jnp.concatenate(split3(vector), axis=0), columns_ref[...], preferred_element_type=f32
    )
    columns = vector.shape[0]
    coeffs = (terms[:columns] + (terms[columns : 2 * columns] + terms[2 * columns :])).T
    return pack_coefficients(coeffs, count)


def join_faces(sent, arrived, live_ref, vector_ref):
    columns, padded = vector_ref.shape[0], sent[0].shape[1]
    for slot in range(4):
        place = slice(slot * padded, (slot + 1) * padded)
        own, other = sent[slot], arrived[ARRIVES.index(slot)]
        total = own[:columns, :] + other[:columns, :]
        vector_ref[:, place] = jnp.where(live_ref[:1, place] > 0.0, total, 0.0)


def first_join_kernel(count, *refs):
    sent, arrived, live_ref = refs[:4], refs[4:8], refs[8]
    vector_ref, coeff_ref, columns_ref, extended_ref, rows_ref = refs[-5:]
    columns, padded = vector_ref.shape[0], sent[0].shape[1]
    group = sent[1].shape[0] - columns
    half = rows_ref.shape[0]
    join_faces(sent, arrived, live_ref, vector_ref)
    rows_ref[...] = jnp.zeros(rows_ref.shape, f32)
    blank = jnp.zeros((columns_ref.shape[1] - group, padded), f32)
    for slot in range(4):
        place = slice(slot * padded, (slot + 1) * padded)
        live = live_ref[:1, place]
        own = sent[slot][columns : columns + group, :] * live
        other = arrived[ARRIVES.index(slot)][columns : columns + group, :] * live
        columns_ref[place, :] = jnp.concatenate([own, blank], axis=0).T.astype(bf16)
        rows_ref[:count, place] = own[:count]
        rows_ref[(1 + slot) * count : (2 + slot) * count, place] = other[:count]
    extended = rows_ref[...].astype(bf16)
    for copy in range(3):
        extended_ref[copy * half : (copy + 1) * half, :] = extended
    write_copies(coeff_ref, coefficients(vector_ref[...], columns_ref, count))


def join_kernel(count, *refs):
    sent, arrived, live_ref, columns_ref = refs[:4], refs[4:8], refs[8], refs[9]
    vector_ref, coeff_ref = refs[-2:]
    join_faces(sent, arrived, live_ref, vector_ref)
    write_copies(coeff_ref, coefficients(vector_ref[...], columns_ref, count))


def projected(coeff_ref, inverse_ref, extended_ref, vector_ref):
    columns, height = vector_ref.shape[0], extended_ref.shape[0] // 3
    pieces = split3(coeff_ref[...])
    factors = jnp.concatenate([pieces[k] for _, k in PRODUCTS], axis=0)
    terms = contract(inverse_ref[...], factors, 1, 0)
    solved = terms[:height, :columns] + jnp.concatenate(
        [
            terms[i * height : (i + 1) * height, columns:]
            for i in range(1, terms.shape[0] // height)
        ],
        axis=1,
    )
    parts = jnp.concatenate(split3(solved), axis=0)
    return vector_ref[...] - contract(parts, extended_ref[...], 0, 0)


def apply_matrix(vector, matrix_ref, face_refs):
    rounded = vector.astype(bf16)
    padded = matrix_ref.shape[1] // 4
    for slot, face_ref in enumerate(face_refs):
        face_ref[...] = contract(
            rounded, matrix_ref[:, slot * padded : (slot + 1) * padded], 1, 0
        )


def start_kernel(coeff_ref, inverse_ref, extended_ref, vector_ref, matrix_ref, *refs):
    residual_ref, face_refs = refs[0], refs[1:]
    residual = projected(coeff_ref, inverse_ref, extended_ref, vector_ref)
    residual_ref[...] = residual
    apply_matrix(residual, matrix_ref, face_refs)


def residual_kernel(coeff_ref, inverse_ref, extended_ref, vector_ref, matrix_ref, old_ref, *refs):
    residual_ref, face_refs = refs[0], refs[1:]
    residual = old_ref[...] - projected(coeff_ref, inverse_ref, extended_ref, vector_ref)
    residual_ref[...] = residual
    apply_matrix(residual, matrix_ref, face_refs)


def first_direction_kernel(alpha, coeff_ref, inverse_ref, extended_ref, vector_ref, matrix_ref, *refs):
    direction_ref, face_refs = refs[0], refs[1:]
    direction = alpha * projected(coeff_ref, inverse_ref, extended_ref, vector_ref)
    direction_ref[...] = direction
    apply_matrix(direction, matrix_ref, face_refs)


def direction_kernel(
    alpha, beta, coeff_ref, inverse_ref, extended_ref, vector_ref, matrix_ref, old_ref, *refs
):
    multipliers_ref, face_refs = refs[0], refs[1:]
    old = old_ref[...]
    preconditioned = projected(coeff_ref, inverse_ref, extended_ref, vector_ref)
    direction = alpha * preconditioned + beta * old
    multipliers_ref[...] = old + direction
    apply_matrix(direction, matrix_ref, face_refs)


def face_order(value, reorder_ref):
    parity = row_parity()
    padded, width = value.shape[1] // 4, reorder_ref.shape[2]
    slots = [value[:, slot * padded : (slot + 1) * padded] for slot in range(4)]
    faces = []
    for face in range(4):
        block = by_parity(
            parity, slots[EVEN_FACES.index(face)], slots[ODD_FACES.index(face)]
        )
        if face in REORDERED:
            faces.append(reorder_exact(block, reorder_ref[REORDERED.index(face)], 0))
        else:
            faces.append(block[:, :width])
    return jnp.concatenate(faces, axis=1)


def last_kernel(coeff_ref, inverse_ref, extended_ref, vector_ref, old_ref, reorder_ref, out_ref):
    residual = old_ref[...] - projected(coeff_ref, inverse_ref, extended_ref, vector_ref)
    out_ref[...] = face_order(residual, reorder_ref)


def multipliers_kernel(vector_ref, reorder_ref, out_ref):
    out_ref[...] = face_order(vector_ref[...], reorder_ref)


def call(kernel, outs, args, hbm=(), after=(), scratch=(), aliases={}):
    vmem = pl.BlockSpec(memory_space=pltpu.VMEM)
    outside = pl.BlockSpec(memory_space=pltpu.HBM)
    anywhere = pl.BlockSpec(memory_space=pl.ANY)
    size = sum(o.size * o.dtype.itemsize for o in (*outs, *args))
    args = [
        pltpu.with_memory_space_constraint(arg, pltpu.HBM) if i in hbm else arg
        for i, arg in enumerate(args)
    ]
    return pl.pallas_call(
        kernel,
        out_shape=tuple(outs),
        in_specs=[
            outside if i in hbm else anywhere if i in after else vmem for i in range(len(args))
        ],
        out_specs=tuple([vmem] * len(outs)),
        scratch_shapes=list(scratch),
        input_output_aliases=aliases,
        compiler_params=pltpu.CompilerParams(vmem_limit_bytes=min(size + (8 << 20), 56 << 20)),
    )(*args)


def local(rows, cols, load, dual_operator, dirichlet, modes, coarse_inverse, face_counts, partners):
    devices = rows * cols
    columns, slots = load.shape[2:]
    width = partners.shape[3]
    padded = round_up(width, 128)
    count = modes.shape[2]
    group = round_up(count, 8)
    height = round_up(5 * count, 16)
    long, short = pack_counts(count)
    packed = columns + columns // (long // short)
    lists = exchanges(rows, cols)
    shape = jax.ShapeDtypeStruct
    vector = shape((columns, 4 * padded), f32)
    faces = [shape((columns, padded), f32)] * 4
    base = columns + group
    lines = inverse_lines(cols, group, rows * count, padded)
    tall_faces = [shape((base + extra, padded), f32) for extra in (lines, 0, 0, lines)]
    matrix = shape((4 * padded, 4 * padded), bf16)
    coeff = shape((devices * long, packed), f32)
    result = shape((columns, slots), f32)
    (alpha_0, _), (alpha_1, beta_1) = chebyshev_coefficients()

    def everywhere(values):
        chunks = values.reshape(devices, long, 1, packed)
        return lax.all_to_all(chunks, ("gy", "gx"), 0, 0).reshape(devices * long, packed)

    raw = shape((slots, slots), bf16)
    wide = pltpu.VMEM((slots, 4 * padded), bf16)
    *sent, live, reorder, smoother, own_part = call(
        load_kernel,
        [
            *tall_faces,
            shape((8, 4 * padded), f32),
            shape((len(REORDERED), padded, width), bf16),
            raw,
            shape(coarse_inverse.shape, f32),
        ],
        (load, modes, partners, face_counts, dirichlet, coarse_inverse),
        (0, 1, 2, 3, 4, 5),
        (),
        [
            pltpu.VMEM((columns, slots), f32),
            pltpu.VMEM((count, slots), bf16),
            pltpu.VMEM((4, width), jnp.int32),
            pltpu.SMEM((1, 4), jnp.int32),
            pltpu.SemaphoreType.DMA((6,)),
        ],
    )
    parts = [own_part] + [
        lax.ppermute(coarse_inverse, "gy", [(b, (b + step) % cols) for b in range(cols)])
        for step in range(1, cols)
    ]
    sent[0], sent[3] = call(
        functools.partial(rows_kernel, count, base),
        [tall_faces[0], tall_faces[3]],
        (sent[0], sent[3], *parts),
        scratch=[pltpu.VMEM((cols, group, rows * count), f32)],
        aliases={0: 0, 1: 1},
    )
    arrived = exchange(sent, lists)
    smoother, operator = call(
        smoother_kernel,
        [matrix, raw],
        (smoother, reorder, dual_operator, sent[0]),
        (2,),
        (3,),
        [wide, pltpu.SemaphoreType.DMA],
    )
    (inverse,) = call(
        functools.partial(inverse_kernel, count, base),
        [shape(((1 + long // short) * height, len(PRODUCTS) * devices * long), bf16)],
        (sent[0], arrived[0], arrived[3], *parts, smoother),
        (),
        (3 + cols,),
        [pltpu.VMEM((cols, height, rows * count), f32)],
    )
    current, coeffs, mode_columns, extended = call(
        functools.partial(first_join_kernel, count),
        [vector, coeff, shape((4 * padded, 128), bf16), shape((3 * height, 4 * padded), bf16)],
        (*sent, *arrived, live, inverse),
        (),
        (9,),
        [pltpu.VMEM((height, 4 * padded), f32)],
    )

    def join(sent, *before, last=False):
        arrived = exchange(sent, lists)
        current, coeffs = call(
            functools.partial(join_kernel, count),
            [vector, coeff],
            (*sent, *arrived, live, mode_columns, *before),
            (10,) if last else (),
            (10,),
        )
        return everywhere(coeffs), inverse, extended, current

    residual, *sent = call(
        start_kernel,
        [vector, *faces],
        (everywhere(coeffs), inverse, extended, current, smoother),
    )
    (operator,) = call(
        operator_kernel, [matrix], (operator, reorder, residual), (), (2,), [wide]
    )
    direction, *sent = call(
        functools.partial(first_direction_kernel, alpha_0),
        [vector, *faces],
        (*join(sent, operator), operator),
    )
    residual, *sent = call(
        residual_kernel, [vector, *faces], (*join(sent), smoother, residual)
    )
    multipliers, *sent = call(
        functools.partial(direction_kernel, alpha_1, beta_1),
        [vector, *faces],
        (*join(sent), operator, direction),
    )
    (multipliers,) = call(multipliers_kernel, [result], (multipliers, reorder))
    (residual,) = call(
        last_kernel, [result], (*join(sent, multipliers, last=True), residual, reorder)
    )
    return (multipliers[None, None], residual[None, None])


def solution(mesh):
    return jax.shard_map(
        functools.partial(local, mesh.shape["gx"], mesh.shape["gy"]),
        mesh=mesh,
        in_specs=(
            P("gx", "gy", None, None),
            P("gx", "gy", None, None),
            P("gx", "gy", None, None),
            P("gx", "gy", None, None),
            P("gx", None, "gy", None),
            P("gx", "gy", None),
            P("gx", "gy", None, None),
        ),
        out_specs=(P("gx", "gy", None, None), P("gx", "gy", None, None)),
        check_vma=False,
    )
```

```python
import functools

import jax
import jax.numpy as jnp
from jax import lax
from jax.experimental import pallas as pl
from jax.experimental.pallas import tpu as pltpu
from jax.sharding import PartitionSpec as P

f32 = jnp.float32
bf16 = jnp.bfloat16
precise = lax.Precision.HIGHEST
spectrum_low = 0.5
spectrum_high = 4.0

EVEN_FACES = (3, 0, 2, 1)
ODD_FACES = (2, 1, 3, 0)
ARRIVES = (2, 1, 0, 3)
REORDERED = (0, 2)


PRODUCTS = ((0, 0), (0, 1), (1, 0), (1, 1), (0, 2), (2, 0))


def round_up(value, unit):
    return -(-value // unit) * unit


def exchanges(rows, cols):
    def pairs(target):
        return [
            (a * cols + b, target(a, b)[0] * cols + target(a, b)[1])
            for a in range(rows)
            for b in range(cols)
        ]

    def along(a, b, step):
        return (a, b + step) if 0 <= b + step < cols else (a ^ 1, b)

    return (
        pairs(lambda a, b: along(a, b, -1 if a % 2 else 1)),
        pairs(lambda a, b: ((a + 1 if a % 2 else a - 1) % rows, b)),
        pairs(lambda a, b: along(a, b, 1 if a % 2 else -1)),
        pairs(lambda a, b: (a ^ 1, b)),
    )


def column_met(here, step, cols):
    if cols & (cols - 1) == 0:
        return here ^ step
    return (here + cols - step) % cols


def exchange(values, lists):
    return [lax.ppermute(value, ("gx", "gy"), pairs) for value, pairs in zip(values, lists)]


def chebyshev_coefficients():
    center = (spectrum_high + spectrum_low) / 2.0
    radius = (spectrum_high - spectrum_low) / 2.0
    center_ratio = center / radius
    factor_prev = 1.0 / center_ratio
    result = [(1.0 / center, 0.0)]
    factor = 1.0 / (2.0 * center_ratio - factor_prev)
    result.append((2.0 * factor / radius, factor * factor_prev))
    return result


def split3(value):
    high = value.astype(bf16)
    rest = value - high.astype(f32)
    middle = rest.astype(bf16)
    low = (rest - middle.astype(f32)).astype(bf16)
    return high, middle, low


def contract(left, right, left_dim, right_dim, precision=None):
    return lax.dot_general(
        left,
        right,
        (((left_dim,), (right_dim,)), ((), ())),
        precision=precision,
        preferred_element_type=f32,
    )


def by_parity(parity, even, odd):
    return jnp.where(parity == 0, even, odd)


def slot_of(face, parity):
    return by_parity(parity, EVEN_FACES.index(face), ODD_FACES.index(face))


def slots_from(faces, parity):
    return [by_parity(parity, faces[EVEN_FACES[j]], faces[ODD_FACES[j]]) for j in range(4)]


def reorder_matrix(place, padded):
    rows = lax.broadcasted_iota(jnp.int32, (padded, place.shape[1]), 0)
    return jnp.where(rows == place, 1.0, 0.0).astype(bf16)


def widened(value, padded):
    blank = jnp.zeros((value.shape[0], padded - value.shape[1]), value.dtype)
    return jnp.concatenate([value, blank], axis=1)


def reorder_exact(value, matrix, dim):
    count = value.shape[0]
    parts = contract(jnp.concatenate(split3(value), axis=0), matrix, 1, dim)
    return parts[:count] + (parts[count : 2 * count] + parts[2 * count :])


def row_parity():
    return lax.rem(lax.axis_index("gx"), 2)


def pack_counts(count):
    long = count * 3 // 4
    return long, count - long


def pack_coefficients(coeffs, count):
    long, short = pack_counts(count)
    pieces = long // short
    piece = coeffs.shape[1] // pieces
    tail = coeffs[long:count]
    side = jnp.concatenate([tail[:, i * piece : (i + 1) * piece] for i in range(pieces)], axis=0)
    return jnp.concatenate([coeffs[:long], side], axis=1)


def packed_shape(columns, width, padded):
    tail = width % 128
    free = 128 - tail
    pieces = tail // free if tail else 0
    if padded != 256 or not pieces or tail % free or columns % (8 * (pieces + 1)):
        return columns, padded
    return columns + columns * pieces // (pieces + 1), 128


def packed_parts(columns, rows):
    kept = rows - columns
    moved = columns - kept
    pieces = kept // moved
    free = 128 // (pieces + 1)
    return kept, moved, pieces, free, 128 - free


def pack_face(value, shape):
    if value.shape == shape:
        return value
    kept, _, pieces, free, tail = packed_parts(value.shape[0], shape[0])
    first, second = value[:, :128], value[:, 128:]
    lowest = second[kept:]
    side = [pltpu.roll(lowest, tail - i * free, 1) for i in range(pieces)]
    lanes = lax.broadcasted_iota(jnp.int32, (kept, 128), 1)
    second = jnp.where(lanes < tail, second[:kept], jnp.concatenate(side, axis=0))
    return jnp.concatenate([first, second], axis=0)


def unpack_face(value, columns):
    if value.shape[0] == columns:
        return value
    _, moved, pieces, free, tail = packed_parts(columns, value.shape[0])
    first, second = value[:columns], value[columns:]
    lanes = lax.broadcasted_iota(jnp.int32, (moved, 128), 1)
    lowest = jnp.zeros((moved, 128), value.dtype)
    for i in range(pieces):
        piece = pltpu.roll(second[i * moved : (i + 1) * moved], 128 - tail + i * free, 1)
        inside = (lanes >= i * free) & (lanes < (i + 1) * free)
        lowest = jnp.where(inside, piece, lowest)
    second = jnp.concatenate([second, lowest], axis=0)
    return jnp.concatenate([first, second], axis=1)


def write_copies(out_ref, value):
    height = value.shape[0]
    copies = out_ref.shape[0] // height
    together = 8 if copies % 8 == 0 else 1
    block = jnp.concatenate([value] * together, axis=0)
    for i in range(copies // together):
        out_ref[i * together * height : (i + 1) * together * height, :] = block


def inverse_places(index, group, length, padded):
    block = round_up(length, 128)
    beside = max(padded // block, 1)
    below = -(-length // padded)
    return [
        (
            ((index // beside) * below + part) * group,
            (index % beside) * block,
            slice(part * padded, min(length, (part + 1) * padded)),
        )
        for part in range(below)
    ]


def inverse_lines(cols, group, length, padded):
    return max(
        place[0] + group
        for index in range(cols)
        for place in inverse_places(index, group, length, padded)
    )


def load_kernel(
    load_hbm, modes_hbm, partners_hbm, counts_hbm, matrix_hbm, inverse_hbm,
    slot_0, slot_1, slot_2, slot_3, live_ref, reorder_ref, matrix_ref, inverse_ref,
    load_ref, modes_ref, partners_ref, counts_ref, sems,
):
    copies = [
        pltpu.make_async_copy(source, target, sems.at[i])
        for i, (source, target) in enumerate(
            (
                (partners_hbm.at[0, 0], partners_ref),
                (load_hbm.at[0, 0], load_ref),
                (modes_hbm.at[0, 0], modes_ref),
                (counts_hbm.at[0], counts_ref),
                (inverse_hbm, inverse_ref),
                (matrix_hbm.at[0, 0], matrix_ref),
            )
        )
    ]
    for copy in copies:
        copy.start()
    for copy in copies[:4]:
        copy.wait()
    parity = row_parity()
    width = partners_ref.shape[1]
    columns, count = load_ref.shape[0], modes_ref.shape[0]
    padded = slot_0.shape[1]
    values, modes = [], []
    for face in range(4):
        place = slice(face * width, (face + 1) * width)
        if face in REORDERED:
            matrix = reorder_matrix(partners_ref[face : face + 1, :], padded)
            reorder_ref[REORDERED.index(face)] = matrix
            values.append(reorder_exact(load_ref[:, place], matrix, 1))
            modes.append(contract(modes_ref[:, place], matrix, 1, 1))
        else:
            values.append(widened(load_ref[:, place], padded))
            modes.append(widened(modes_ref[:, place], padded).astype(f32))
    values, modes = slots_from(values, parity), slots_from(modes, parity)
    for slot, slot_ref in enumerate((slot_0, slot_1, slot_2, slot_3)):
        slot_ref[columns:, :] = jnp.zeros((slot_ref.shape[0] - columns, padded), f32)
        slot_ref[:columns, :] = values[slot]
        slot_ref[columns : columns + count, :] = modes[slot]
        live = by_parity(
            parity, counts_ref[0, EVEN_FACES[slot]], counts_ref[0, ODD_FACES[slot]]
        )
        places = lax.broadcasted_iota(jnp.int32, (live_ref.shape[0], padded), 1)
        live_ref[:, slot * padded : (slot + 1) * padded] = jnp.where(places < live, 1.0, 0.0)
    for copy in copies[4:]:
        copy.wait()


def reorder_operator(matrix_ref, reorder_ref, out_ref, columns_ref):
    parity = row_parity()
    width, padded = matrix_ref.shape[1] // 4, out_ref.shape[1] // 4

    def slot_place(face):
        return pl.ds(pl.multiple_of(slot_of(face, parity) * padded, padded), padded)

    for face in range(4):
        block = matrix_ref[:, face * width : (face + 1) * width]
        if face in REORDERED:
            block = contract(block, reorder_ref[REORDERED.index(face)], 1, 1).astype(bf16)
        else:
            block = widened(block, padded)
        columns_ref[:, slot_place(face)] = block
    for face in range(4):
        block = columns_ref[face * width : (face + 1) * width, :]
        if face in REORDERED:
            block = contract(reorder_ref[REORDERED.index(face)], block, 1, 0).astype(bf16)
        else:
            blank = jnp.zeros((padded - width, block.shape[1]), bf16)
            block = jnp.concatenate([block, blank], axis=0)
        out_ref[slot_place(face), :] = block


def operator_kernel(matrix_ref, reorder_ref, after_hbm, out_ref, columns_ref):
    reorder_operator(matrix_ref, reorder_ref, out_ref, columns_ref)


def rows_kernel(count, base, *refs):
    part_refs, (first_ref, second_ref, rows_ref) = refs[2:-4], refs[-3:]
    cols, here = len(part_refs), lax.axis_index("gy")
    group, length = rows_ref.shape[1:]
    rows_ref[...] = jnp.zeros(rows_ref.shape, f32)
    for step, part_ref in enumerate(part_refs):
        source = column_met(here, step, cols)
        rows_ref[source, :count, :] = part_ref[0, pl.ds(here * count, count), 0, :]
    for face_ref in (first_ref, second_ref):
        for e in range(cols):
            for line, lane, part in inverse_places(e, group, length, face_ref.shape[1]):
                face_ref[
                    base + line : base + line + group, lane : lane + part.stop - part.start
                ] = rows_ref[e, :, part]


def inverse_kernel(count, base, *refs):
    face_refs = refs[:3]
    part_refs, (out_ref, rows_ref) = refs[3:-3], refs[-2:]
    cols = len(part_refs)
    parity, here = row_parity(), lax.axis_index("gy")
    north, south = jnp.minimum(here + 1, cols - 1), jnp.maximum(here - 1, 0)
    length = rows_ref.shape[2]
    group = round_up(count, 8)
    rows, height = length // count, rows_ref.shape[1]
    long, short = pack_counts(count)
    rows_ref[...] = jnp.zeros(rows_ref.shape, f32)
    for e in range(cols):
        for i, ref in zip((0, 2, 4), face_refs):
            for line, lane, part in inverse_places(e, group, length, ref.shape[1]):
                rows_ref[e, i * count : (i + 1) * count, part] = ref[
                    base + line : base + line + count, lane : lane + part.stop - part.start
                ]
    for step, part_ref in enumerate(part_refs):
        source_col = column_met(here, step, cols)
        for i, row in ((1, jnp.where(parity == 0, north, south)), (3, jnp.where(parity == 0, south, north))):
            rows_ref[source_col, i * count : (i + 1) * count, :] = part_ref[
                0, pl.ds(row * count, count), 0, :
            ]
    wide = rows * long
    source = lax.broadcasted_iota(jnp.int32, (length, wide), 0)
    target = lax.broadcasted_iota(jnp.int32, (length, wide), 1)
    source_row, source_mode = lax.div(source, count), lax.rem(source, count)
    target_row, target_place = lax.div(target, long), lax.rem(target, long)
    same = source_row == target_row
    places = [jnp.where(same & (source_mode == target_place), 1.0, 0.0).astype(bf16)]
    for part in range(long // short):
        wanted = target_place - part * short
        inside = (wanted >= 0) & (wanted < short)
        places.append(
            jnp.where(same & inside & (source_mode == long + wanted), 1.0, 0.0).astype(bf16)
        )
    place = jnp.concatenate(places, axis=1)
    gathered = [[] for _ in places]
    for e in range(cols):
        pieces = jnp.concatenate(split3(rows_ref[e]), axis=0)
        moved = contract(pieces, place, 1, 0)
        for part in range(len(places)):
            gathered[part].append(moved[:, part * wide : (part + 1) * wide])
    for part, pieces in enumerate(gathered):
        high, middle, low = (
            jnp.concatenate([p[k * height : (k + 1) * height] for p in pieces], axis=1)
            for k in range(3)
        )
        factors = [(high, middle, low)[k] for k, _ in PRODUCTS]
        out_ref[part * height : (part + 1) * height, :] = jnp.concatenate(factors, axis=1).astype(
            bf16
        )


def coefficients(vector, columns_ref, count):
    terms = jnp.dot(
        jnp.concatenate(split3(vector), axis=0), columns_ref[...], preferred_element_type=f32
    )
    columns = vector.shape[0]
    coeffs = (terms[:columns] + (terms[columns : 2 * columns] + terms[2 * columns :])).T
    return pack_coefficients(coeffs, count)


def join_faces(sent, arrived, live_ref, vector_ref):
    columns, padded = vector_ref.shape[0], vector_ref.shape[1] // 4
    for slot in range(4):
        place = slice(slot * padded, (slot + 1) * padded)
        own, other = sent[slot], arrived[ARRIVES.index(slot)]
        height = columns if own.shape[1] == padded else own.shape[0]
        total = unpack_face(own[:height, :] + other[:height, :], columns)
        vector_ref[:, place] = jnp.where(live_ref[:1, place] > 0.0, total, 0.0)


def first_join_kernel(count, *refs):
    sent, arrived, live_ref = refs[:4], refs[4:8], refs[8]
    vector_ref, coeff_ref, columns_ref, extended_ref, rows_ref = refs[-5:]
    columns, padded = vector_ref.shape[0], sent[0].shape[1]
    group = sent[0].shape[0] - columns
    half = rows_ref.shape[0]
    join_faces(sent, arrived, live_ref, vector_ref)
    rows_ref[...] = jnp.zeros(rows_ref.shape, f32)
    blank = jnp.zeros((columns_ref.shape[1] - group, padded), f32)
    for slot in range(4):
        place = slice(slot * padded, (slot + 1) * padded)
        live = live_ref[:1, place]
        own = sent[slot][columns : columns + group, :] * live
        other = arrived[ARRIVES.index(slot)][columns : columns + group, :] * live
        columns_ref[place, :] = jnp.concatenate([own, blank], axis=0).T.astype(bf16)
        rows_ref[:count, place] = own[:count]
        rows_ref[(1 + slot) * count : (2 + slot) * count, place] = other[:count]
    extended = rows_ref[...].astype(bf16)
    for copy in range(3):
        extended_ref[copy * half : (copy + 1) * half, :] = extended
    write_copies(coeff_ref, coefficients(vector_ref[...], columns_ref, count))


def join_kernel(count, *refs):
    sent, arrived, live_ref, columns_ref = refs[:4], refs[4:8], refs[8], refs[9]
    vector_ref, coeff_ref = refs[-2:]
    columns, padded = vector_ref.shape[0], vector_ref.shape[1] // 4
    terms = jnp.zeros((3 * columns, columns_ref.shape[1]), f32)
    for slot in range(4):
        place = slice(slot * padded, (slot + 1) * padded)
        total = unpack_face(sent[slot][...] + arrived[ARRIVES.index(slot)][...], columns)
        total = jnp.where(live_ref[:1, place] > 0.0, total, 0.0)
        vector_ref[:, place] = total
        pieces = jnp.concatenate(split3(total), axis=0)
        terms = terms + jnp.dot(pieces, columns_ref[place, :], preferred_element_type=f32)
    coeffs = terms[:columns] + (terms[columns : 2 * columns] + terms[2 * columns :])
    write_copies(coeff_ref, pack_coefficients(coeffs.T, count))


def projected(coeff_ref, inverse_ref, extended_ref, vector_ref):
    columns, height = vector_ref.shape[0], extended_ref.shape[0] // 3
    pieces = split3(coeff_ref[...])
    factors = jnp.concatenate([pieces[k] for _, k in PRODUCTS], axis=0)
    terms = contract(inverse_ref[...], factors, 1, 0)
    solved = terms[:height, :columns] + jnp.concatenate(
        [
            terms[i * height : (i + 1) * height, columns:]
            for i in range(1, terms.shape[0] // height)
        ],
        axis=1,
    )
    parts = jnp.concatenate(split3(solved), axis=0)
    return vector_ref[...] - contract(parts, extended_ref[...], 0, 0)


def apply_matrix(vector, matrix_ref, face_refs):
    rounded = vector.astype(bf16)
    padded = matrix_ref.shape[1] // 4
    for slot, face_ref in enumerate(face_refs):
        product = contract(rounded, matrix_ref[:, slot * padded : (slot + 1) * padded], 1, 0)
        face_ref[...] = pack_face(product, face_ref.shape)


def start_kernel(coeff_ref, inverse_ref, extended_ref, vector_ref, matrix_ref, *refs):
    residual_ref, face_refs = refs[0], refs[1:]
    residual = projected(coeff_ref, inverse_ref, extended_ref, vector_ref)
    residual_ref[...] = residual
    apply_matrix(residual, matrix_ref, face_refs)


def residual_kernel(coeff_ref, inverse_ref, extended_ref, vector_ref, matrix_ref, old_ref, *refs):
    residual_ref, face_refs = refs[0], refs[1:]
    residual = old_ref[...] - projected(coeff_ref, inverse_ref, extended_ref, vector_ref)
    residual_ref[...] = residual
    apply_matrix(residual, matrix_ref, face_refs)


def first_direction_kernel(alpha, coeff_ref, inverse_ref, extended_ref, vector_ref, matrix_ref, *refs):
    direction_ref, face_refs = refs[0], refs[1:]
    direction = alpha * projected(coeff_ref, inverse_ref, extended_ref, vector_ref)
    direction_ref[...] = direction
    apply_matrix(direction, matrix_ref, face_refs)


def direction_kernel(
    alpha, beta, coeff_ref, inverse_ref, extended_ref, vector_ref, matrix_ref, old_ref, *refs
):
    multipliers_ref, face_refs = refs[0], refs[1:]
    old = old_ref[...]
    preconditioned = projected(coeff_ref, inverse_ref, extended_ref, vector_ref)
    direction = alpha * preconditioned + beta * old
    multipliers_ref[...] = old + direction
    apply_matrix(direction, matrix_ref, face_refs)


def face_order(value, reorder_ref):
    parity = row_parity()
    padded, width = value.shape[1] // 4, reorder_ref.shape[2]
    slots = [value[:, slot * padded : (slot + 1) * padded] for slot in range(4)]
    faces = []
    for face in range(4):
        block = by_parity(
            parity, slots[EVEN_FACES.index(face)], slots[ODD_FACES.index(face)]
        )
        if face in REORDERED:
            faces.append(reorder_exact(block, reorder_ref[REORDERED.index(face)], 0))
        else:
            faces.append(block[:, :width])
    return jnp.concatenate(faces, axis=1)


def last_kernel(
    coeff_ref, inverse_ref, extended_ref, vector_ref, old_ref, reorder_ref, out_hbm, out_ref, sems
):
    residual = old_ref[...] - projected(coeff_ref, inverse_ref, extended_ref, vector_ref)
    parts = sems.shape[0]
    share = residual.shape[0] // parts
    copies = []
    for i in range(parts):
        out_ref[i] = face_order(residual[i * share : (i + 1) * share], reorder_ref)
        target = out_hbm.at[pl.ds(i * share, share)]
        copies.append(pltpu.make_async_copy(out_ref.at[i], target, sems.at[i]))
        copies[-1].start()
    for copy in copies:
        copy.wait()


def multipliers_kernel(vector_ref, reorder_ref, out_ref):
    out_ref[...] = face_order(vector_ref[...], reorder_ref)


def call(kernel, outs, args, hbm=(), after=(), scratch=(), aliases={}, out_space=pltpu.VMEM):
    vmem = pl.BlockSpec(memory_space=pltpu.VMEM)
    outside = pl.BlockSpec(memory_space=pltpu.HBM)
    anywhere = pl.BlockSpec(memory_space=pl.ANY)
    size = sum(o.size * o.dtype.itemsize for o in (*outs, *args))
    args = [
        pltpu.with_memory_space_constraint(arg, pltpu.HBM) if i in hbm else arg
        for i, arg in enumerate(args)
    ]
    return pl.pallas_call(
        kernel,
        out_shape=tuple(outs),
        in_specs=[
            outside if i in hbm else anywhere if i in after else vmem for i in range(len(args))
        ],
        out_specs=tuple([pl.BlockSpec(memory_space=out_space)] * len(outs)),
        scratch_shapes=list(scratch),
        input_output_aliases=aliases,
        compiler_params=pltpu.CompilerParams(vmem_limit_bytes=min(size + (8 << 20), 56 << 20)),
    )(*args)


def local(rows, cols, load, dual_operator, dirichlet, modes, coarse_inverse, face_counts, partners):
    devices = rows * cols
    columns, slots = load.shape[2:]
    width = partners.shape[3]
    padded = round_up(width, 128)
    count = modes.shape[2]
    group = round_up(count, 8)
    height = round_up(5 * count, 16)
    long, short = pack_counts(count)
    packed = columns + columns // (long // short)
    lists = exchanges(rows, cols)
    shape = jax.ShapeDtypeStruct
    vector = shape((columns, 4 * padded), f32)
    faces = [shape(packed_shape(columns, width, padded), f32)] * 4
    base = columns + group
    lines = inverse_lines(cols, group, rows * count, padded)
    tall_faces = [shape((base + extra, padded), f32) for extra in (0, lines, 0, lines)]
    matrix = shape((4 * padded, 4 * padded), bf16)
    coeff = shape((devices * long, packed), f32)
    result = shape((columns, slots), f32)
    (alpha_0, _), (alpha_1, beta_1) = chebyshev_coefficients()

    def everywhere(values):
        chunks = values.reshape(devices, long, 1, packed)
        return lax.all_to_all(chunks, ("gy", "gx"), 0, 0).reshape(devices * long, packed)

    raw = shape((slots, slots), bf16)
    wide = pltpu.VMEM((slots, 4 * padded), bf16)
    *sent, live, reorder, smoother, own_part = call(
        load_kernel,
        [
            *tall_faces,
            shape((8, 4 * padded), f32),
            shape((len(REORDERED), padded, width), bf16),
            raw,
            shape(coarse_inverse.shape, f32),
        ],
        (load, modes, partners, face_counts, dirichlet, coarse_inverse),
        (0, 1, 2, 3, 4, 5),
        (),
        [
            pltpu.VMEM((columns, slots), f32),
            pltpu.VMEM((count, slots), bf16),
            pltpu.VMEM((4, width), jnp.int32),
            pltpu.SMEM((1, 4), jnp.int32),
            pltpu.SemaphoreType.DMA((6,)),
        ],
    )
    parts = [own_part] + [
        lax.ppermute(coarse_inverse, "gy", [(column_met(b, step, cols), b) for b in range(cols)])
        for step in range(1, cols)
    ]
    (smoother,) = call(operator_kernel, [matrix], (smoother, reorder, live), (), (2,), [wide])
    sent[1], sent[3] = call(
        functools.partial(rows_kernel, count, base),
        [tall_faces[1], tall_faces[3]],
        (sent[1], sent[3], *parts, smoother),
        after=(2 + cols,),
        scratch=[pltpu.VMEM((cols, group, rows * count), f32)],
        aliases={0: 0, 1: 1},
    )
    arrived = exchange(sent, lists)
    (operator,) = call(
        operator_kernel, [matrix], (dual_operator[0, 0], reorder, sent[1]), (), (2,), [wide]
    )
    (inverse,) = call(
        functools.partial(inverse_kernel, count, base),
        [shape(((1 + long // short) * height, len(PRODUCTS) * devices * long), bf16)],
        (sent[1], arrived[1], arrived[3], *parts, operator),
        (),
        (3 + cols,),
        [pltpu.VMEM((cols, height, rows * count), f32)],
    )
    current, coeffs, mode_columns, extended = call(
        functools.partial(first_join_kernel, count),
        [vector, coeff, shape((4 * padded, 128), bf16), shape((3 * height, 4 * padded), bf16)],
        (*sent, *arrived, live, inverse),
        (),
        (9,),
        [pltpu.VMEM((height, 4 * padded), f32)],
    )

    def join(sent, *before, last=False):
        arrived = exchange(sent, lists)
        current, coeffs = call(
            functools.partial(join_kernel, count),
            [vector, coeff],
            (*sent, *arrived, live, mode_columns, *before),
            (10,) if last else (),
            (10,),
        )
        return everywhere(coeffs), inverse, extended, current

    residual, *sent = call(
        start_kernel,
        [vector, *faces],
        (everywhere(coeffs), inverse, extended, current, smoother),
    )
    direction, *sent = call(
        functools.partial(first_direction_kernel, alpha_0),
        [vector, *faces],
        (*join(sent), operator),
    )
    residual, *sent = call(
        residual_kernel, [vector, *faces], (*join(sent), smoother, residual)
    )
    multipliers, *sent = call(
        functools.partial(direction_kernel, alpha_1, beta_1),
        [vector, *faces],
        (*join(sent), operator, direction),
    )
    (multipliers,) = call(multipliers_kernel, [result], (multipliers, reorder))
    (residual,) = call(
        last_kernel,
        [result],
        (*join(sent, multipliers, last=True), residual, reorder),
        scratch=[pltpu.VMEM((2, columns // 2, slots), f32), pltpu.SemaphoreType.DMA((2,))],
        out_space=pl.ANY,
    )
    return (multipliers[None, None], residual[None, None])


def solution(mesh):
    return jax.shard_map(
        functools.partial(local, mesh.shape["gx"], mesh.shape["gy"]),
        mesh=mesh,
        in_specs=(
            P("gx", "gy", None, None),
            P("gx", "gy", None, None),
            P("gx", "gy", None, None),
            P("gx", "gy", None, None),
            P("gx", None, "gy", None),
            P("gx", "gy", None),
            P("gx", "gy", None, None),
        ),
        out_specs=(P("gx", "gy", None, None), P("gx", "gy", None, None)),
        check_vma=False,
    )
```

```python
import functools

import jax
import jax.numpy as jnp
from jax import lax
from jax.experimental import pallas as pl
from jax.experimental.pallas import tpu as pltpu
from jax.sharding import PartitionSpec as P

f32 = jnp.float32
bf16 = jnp.bfloat16
precise = lax.Precision.HIGHEST
spectrum_low = 0.5
spectrum_high = 4.0

EVEN_FACES = (3, 0, 2, 1)
ODD_FACES = (2, 1, 3, 0)
ARRIVES = (2, 1, 0, 3)
REORDERED = (0, 2)


PRODUCTS = ((0, 0), (0, 1), (1, 0), (1, 1), (0, 2), (2, 0))


def round_up(value, unit):
    return -(-value // unit) * unit


def exchanges(rows, cols):
    def pairs(target):
        return [
            (a * cols + b, target(a, b)[0] * cols + target(a, b)[1])
            for a in range(rows)
            for b in range(cols)
        ]

    def along(a, b, step):
        return (a, b + step) if 0 <= b + step < cols else (a ^ 1, b)

    return (
        pairs(lambda a, b: along(a, b, -1 if a % 2 else 1)),
        pairs(lambda a, b: ((a + 1 if a % 2 else a - 1) % rows, b)),
        pairs(lambda a, b: along(a, b, 1 if a % 2 else -1)),
        pairs(lambda a, b: (a ^ 1, b)),
    )


def column_met(here, step, cols):
    if cols & (cols - 1) == 0:
        return here ^ step
    return (here + cols - step) % cols


def exchange(values, lists):
    return [lax.ppermute(value, ("gx", "gy"), pairs) for value, pairs in zip(values, lists)]


def chebyshev_coefficients():
    center = (spectrum_high + spectrum_low) / 2.0
    radius = (spectrum_high - spectrum_low) / 2.0
    center_ratio = center / radius
    factor_prev = 1.0 / center_ratio
    result = [(1.0 / center, 0.0)]
    factor = 1.0 / (2.0 * center_ratio - factor_prev)
    result.append((2.0 * factor / radius, factor * factor_prev))
    return result


def split3(value):
    high = value.astype(bf16)
    rest = value - high.astype(f32)
    middle = rest.astype(bf16)
    low = (rest - middle.astype(f32)).astype(bf16)
    return high, middle, low


def contract(left, right, left_dim, right_dim, precision=None):
    return lax.dot_general(
        left,
        right,
        (((left_dim,), (right_dim,)), ((), ())),
        precision=precision,
        preferred_element_type=f32,
    )


def by_parity(parity, even, odd):
    return jnp.where(parity == 0, even, odd)


def slot_of(face, parity):
    return by_parity(parity, EVEN_FACES.index(face), ODD_FACES.index(face))


def slots_from(faces, parity):
    return [by_parity(parity, faces[EVEN_FACES[j]], faces[ODD_FACES[j]]) for j in range(4)]


def reorder_matrix(place, padded):
    rows = lax.broadcasted_iota(jnp.int32, (padded, place.shape[1]), 0)
    return jnp.where(rows == place, 1.0, 0.0).astype(bf16)


def widened(value, padded):
    blank = jnp.zeros((value.shape[0], padded - value.shape[1]), value.dtype)
    return jnp.concatenate([value, blank], axis=1)


def reorder_exact(value, matrix, dim):
    count = value.shape[0]
    parts = contract(jnp.concatenate(split3(value), axis=0), matrix, 1, dim)
    return parts[:count] + (parts[count : 2 * count] + parts[2 * count :])


def row_parity():
    return lax.rem(lax.axis_index("gx"), 2)


def pack_counts(count):
    long = count * 3 // 4
    return long, count - long


def pack_coefficients(coeffs, count):
    long, short = pack_counts(count)
    pieces = long // short
    piece = coeffs.shape[1] // pieces
    tail = coeffs[long:count]
    side = jnp.concatenate([tail[:, i * piece : (i + 1) * piece] for i in range(pieces)], axis=0)
    return jnp.concatenate([coeffs[:long], side], axis=1)


def packed_shape(columns, width, padded):
    tail = width % 128
    free = 128 - tail
    pieces = tail // free if tail else 0
    if padded != 256 or not pieces or tail % free or columns % (8 * (pieces + 1)):
        return columns, padded
    return columns + columns * pieces // (pieces + 1), 128


def packed_parts(columns, rows):
    kept = rows - columns
    moved = columns - kept
    pieces = kept // moved
    free = 128 // (pieces + 1)
    return kept, moved, pieces, free, 128 - free


def pack_face(value, shape):
    if value.shape == shape:
        return value
    kept, _, pieces, free, tail = packed_parts(value.shape[0], shape[0])
    first, second = value[:, :128], value[:, 128:]
    lowest = second[kept:]
    side = [pltpu.roll(lowest, tail - i * free, 1) for i in range(pieces)]
    lanes = lax.broadcasted_iota(jnp.int32, (kept, 128), 1)
    second = jnp.where(lanes < tail, second[:kept], jnp.concatenate(side, axis=0))
    return jnp.concatenate([first, second], axis=0)


def unpack_face(value, columns):
    if value.shape[0] == columns:
        return value
    _, moved, pieces, free, tail = packed_parts(columns, value.shape[0])
    first, second = value[:columns], value[columns:]
    lanes = lax.broadcasted_iota(jnp.int32, (moved, 128), 1)
    lowest = jnp.zeros((moved, 128), value.dtype)
    for i in range(pieces):
        piece = pltpu.roll(second[i * moved : (i + 1) * moved], 128 - tail + i * free, 1)
        inside = (lanes >= i * free) & (lanes < (i + 1) * free)
        lowest = jnp.where(inside, piece, lowest)
    second = jnp.concatenate([second, lowest], axis=0)
    return jnp.concatenate([first, second], axis=1)


def write_places(out_ref, count):
    long, short = pack_counts(count)
    length = out_ref.shape[0]
    wide = length // count * long
    source = lax.broadcasted_iota(jnp.int32, (length, wide), 0)
    target = lax.broadcasted_iota(jnp.int32, (length, wide), 1)
    source_row, source_mode = lax.div(source, count), lax.rem(source, count)
    target_row, target_place = lax.div(target, long), lax.rem(target, long)
    same = source_row == target_row
    places = [jnp.where(same & (source_mode == target_place), 1.0, 0.0).astype(bf16)]
    for part in range(long // short):
        wanted = target_place - part * short
        inside = (wanted >= 0) & (wanted < short)
        places.append(
            jnp.where(same & inside & (source_mode == long + wanted), 1.0, 0.0).astype(bf16)
        )
    out_ref[...] = jnp.concatenate(places, axis=1)


def write_copies(out_ref, value):
    height = value.shape[0]
    copies = out_ref.shape[0] // height
    together = 8 if copies % 8 == 0 else 1
    block = jnp.concatenate([value] * together, axis=0)
    for i in range(copies // together):
        out_ref[i * together * height : (i + 1) * together * height, :] = block


def inverse_places(index, group, length, padded):
    block = round_up(length, 128)
    beside = max(padded // block, 1)
    below = -(-length // padded)
    return [
        (
            ((index // beside) * below + part) * group,
            (index % beside) * block,
            slice(part * padded, min(length, (part + 1) * padded)),
        )
        for part in range(below)
    ]


def inverse_lines(cols, group, length, padded):
    return max(
        place[0] + group
        for index in range(cols)
        for place in inverse_places(index, group, length, padded)
    )


def load_kernel(
    load_hbm, modes_hbm, partners_hbm, counts_hbm, matrix_hbm, inverse_hbm,
    slot_0, slot_1, slot_2, slot_3, live_ref, reorder_ref, places_ref, matrix_ref, inverse_ref,
    load_ref, modes_ref, partners_ref, counts_ref, sems,
):
    copies = [
        pltpu.make_async_copy(source, target, sems.at[i])
        for i, (source, target) in enumerate(
            (
                (partners_hbm.at[0, 0], partners_ref),
                (load_hbm.at[0, 0], load_ref),
                (modes_hbm.at[0, 0], modes_ref),
                (counts_hbm.at[0], counts_ref),
                (inverse_hbm, inverse_ref),
                (matrix_hbm.at[0, 0], matrix_ref),
            )
        )
    ]
    for copy in copies:
        copy.start()
    for copy in copies[:4]:
        copy.wait()
    parity = row_parity()
    width = partners_ref.shape[1]
    columns, count = load_ref.shape[0], modes_ref.shape[0]
    padded = slot_0.shape[1]
    values, modes = [], []
    for face in range(4):
        place = slice(face * width, (face + 1) * width)
        if face in REORDERED:
            matrix = reorder_matrix(partners_ref[face : face + 1, :], padded)
            reorder_ref[REORDERED.index(face)] = matrix
            values.append(reorder_exact(load_ref[:, place], matrix, 1))
            modes.append(contract(modes_ref[:, place], matrix, 1, 1))
        else:
            values.append(widened(load_ref[:, place], padded))
            modes.append(widened(modes_ref[:, place], padded).astype(f32))
    values, modes = slots_from(values, parity), slots_from(modes, parity)
    for slot, slot_ref in enumerate((slot_0, slot_1, slot_2, slot_3)):
        slot_ref[columns:, :] = jnp.zeros((slot_ref.shape[0] - columns, padded), f32)
        slot_ref[:columns, :] = values[slot]
        slot_ref[columns : columns + count, :] = modes[slot]
        live = by_parity(
            parity, counts_ref[0, EVEN_FACES[slot]], counts_ref[0, ODD_FACES[slot]]
        )
        places = lax.broadcasted_iota(jnp.int32, (live_ref.shape[0], padded), 1)
        live_ref[:, slot * padded : (slot + 1) * padded] = jnp.where(places < live, 1.0, 0.0)
    write_places(places_ref, count)
    for copy in copies[4:]:
        copy.wait()


def reorder_operator(matrix_ref, reorder_ref, out_ref, columns_ref):
    parity = row_parity()
    width, padded = matrix_ref.shape[1] // 4, out_ref.shape[1] // 4

    def slot_place(face):
        return pl.ds(pl.multiple_of(slot_of(face, parity) * padded, padded), padded)

    for face in range(4):
        block = matrix_ref[:, face * width : (face + 1) * width]
        if face in REORDERED:
            block = contract(block, reorder_ref[REORDERED.index(face)], 1, 1).astype(bf16)
        else:
            block = widened(block, padded)
        columns_ref[:, slot_place(face)] = block
    for face in range(4):
        block = columns_ref[face * width : (face + 1) * width, :]
        if face in REORDERED:
            block = contract(reorder_ref[REORDERED.index(face)], block, 1, 0).astype(bf16)
        else:
            blank = jnp.zeros((padded - width, block.shape[1]), bf16)
            block = jnp.concatenate([block, blank], axis=0)
        out_ref[slot_place(face), :] = block


def operator_kernel(matrix_ref, reorder_ref, after_hbm, out_ref, columns_ref):
    reorder_operator(matrix_ref, reorder_ref, out_ref, columns_ref)


def rows_kernel(count, base, *refs):
    part_refs, (first_ref, second_ref, rows_ref) = refs[2:-4], refs[-3:]
    cols, here = len(part_refs), lax.axis_index("gy")
    group, length = rows_ref.shape[1:]
    rows_ref[...] = jnp.zeros(rows_ref.shape, f32)
    for step, part_ref in enumerate(part_refs):
        source = column_met(here, step, cols)
        rows_ref[source, :count, :] = part_ref[0, pl.ds(here * count, count), 0, :]
    for face_ref in (first_ref, second_ref):
        for e in range(cols):
            for line, lane, part in inverse_places(e, group, length, face_ref.shape[1]):
                face_ref[
                    base + line : base + line + group, lane : lane + part.stop - part.start
                ] = rows_ref[e, :, part]


def inverse_kernel(count, base, *refs):
    face_refs, places_ref = refs[:3], refs[3]
    part_refs, (out_ref, rows_ref) = refs[4:-3], refs[-2:]
    cols = len(part_refs)
    parity, here = row_parity(), lax.axis_index("gy")
    north, south = jnp.minimum(here + 1, cols - 1), jnp.maximum(here - 1, 0)
    length = rows_ref.shape[2]
    group = round_up(count, 8)
    rows, height = length // count, rows_ref.shape[1]
    long, short = pack_counts(count)
    rows_ref[...] = jnp.zeros(rows_ref.shape, f32)
    for e in range(cols):
        for i, ref in zip((0, 2, 4), face_refs):
            for line, lane, part in inverse_places(e, group, length, ref.shape[1]):
                rows_ref[e, i * count : (i + 1) * count, part] = ref[
                    base + line : base + line + count, lane : lane + part.stop - part.start
                ]
    for step, part_ref in enumerate(part_refs):
        source_col = column_met(here, step, cols)
        for i, row in ((1, jnp.where(parity == 0, north, south)), (3, jnp.where(parity == 0, south, north))):
            rows_ref[source_col, i * count : (i + 1) * count, :] = part_ref[
                0, pl.ds(row * count, count), 0, :
            ]
    ratio = 1 + long // short
    wide = rows * long
    gathered = [[] for _ in range(ratio)]
    for e in range(cols):
        pieces = jnp.concatenate(split3(rows_ref[e]), axis=0)
        moved = contract(pieces, places_ref[...], 1, 0)
        for part in range(ratio):
            gathered[part].append(moved[:, part * wide : (part + 1) * wide])
    for part, pieces in enumerate(gathered):
        high, middle, low = (
            jnp.concatenate([p[k * height : (k + 1) * height] for p in pieces], axis=1)
            for k in range(3)
        )
        factors = [(high, middle, low)[k] for k, _ in PRODUCTS]
        out_ref[part * height : (part + 1) * height, :] = jnp.concatenate(factors, axis=1).astype(
            bf16
        )


def coefficients(vector, columns_ref, count):
    padded = vector.shape[1] // 4
    terms = jnp.zeros((3 * vector.shape[0], columns_ref.shape[1]), f32)
    for slot in range(4):
        place = slice(slot * padded, (slot + 1) * padded)
        pieces = jnp.concatenate(split3(vector[:, place]), axis=0)
        terms = terms + jnp.dot(pieces, columns_ref[place, :], preferred_element_type=f32)
    columns = vector.shape[0]
    coeffs = (terms[:columns] + (terms[columns : 2 * columns] + terms[2 * columns :])).T
    return pack_coefficients(coeffs, count)


def join_faces(sent, arrived, live_ref, vector_ref):
    columns, padded = vector_ref.shape[0], vector_ref.shape[1] // 4
    for slot in range(4):
        place = slice(slot * padded, (slot + 1) * padded)
        own, other = sent[slot], arrived[ARRIVES.index(slot)]
        height = columns if own.shape[1] == padded else own.shape[0]
        total = unpack_face(own[:height, :] + other[:height, :], columns)
        vector_ref[:, place] = jnp.where(live_ref[:1, place] > 0.0, total, 0.0)


def first_join_kernel(count, *refs):
    sent, arrived, live_ref = refs[:4], refs[4:8], refs[8]
    vector_ref, coeff_ref, columns_ref, extended_ref, rows_ref = refs[-5:]
    columns, padded = vector_ref.shape[0], sent[0].shape[1]
    group = sent[0].shape[0] - columns
    half = rows_ref.shape[0]
    join_faces(sent, arrived, live_ref, vector_ref)
    rows_ref[...] = jnp.zeros(rows_ref.shape, f32)
    blank = jnp.zeros((columns_ref.shape[1] - group, padded), f32)
    for slot in range(4):
        place = slice(slot * padded, (slot + 1) * padded)
        live = live_ref[:1, place]
        own = sent[slot][columns : columns + group, :] * live
        other = arrived[ARRIVES.index(slot)][columns : columns + group, :] * live
        columns_ref[place, :] = jnp.concatenate([own, blank], axis=0).T.astype(bf16)
        rows_ref[:count, place] = own[:count]
        rows_ref[(1 + slot) * count : (2 + slot) * count, place] = other[:count]
    extended = rows_ref[...].astype(bf16)
    for copy in range(3):
        extended_ref[copy * half : (copy + 1) * half, :] = extended
    write_copies(coeff_ref, coefficients(vector_ref[...], columns_ref, count))


def join_kernel(count, *refs):
    sent, arrived, live_ref, columns_ref = refs[:4], refs[4:8], refs[8], refs[9]
    vector_ref, coeff_ref = refs[-2:]
    columns, padded = vector_ref.shape[0], vector_ref.shape[1] // 4
    terms = jnp.zeros((3 * columns, columns_ref.shape[1]), f32)
    for slot in range(4):
        place = slice(slot * padded, (slot + 1) * padded)
        total = unpack_face(sent[slot][...] + arrived[ARRIVES.index(slot)][...], columns)
        total = jnp.where(live_ref[:1, place] > 0.0, total, 0.0)
        vector_ref[:, place] = total
        pieces = jnp.concatenate(split3(total), axis=0)
        terms = terms + jnp.dot(pieces, columns_ref[place, :], preferred_element_type=f32)
    coeffs = terms[:columns] + (terms[columns : 2 * columns] + terms[2 * columns :])
    write_copies(coeff_ref, pack_coefficients(coeffs.T, count))


def projected(coeff_ref, inverse_ref, extended_ref, vector_ref):
    columns, height = vector_ref.shape[0], extended_ref.shape[0] // 3
    pieces = split3(coeff_ref[...])
    factors = jnp.concatenate([pieces[k] for _, k in PRODUCTS], axis=0)
    terms = contract(inverse_ref[...], factors, 1, 0)
    solved = terms[:height, :columns] + jnp.concatenate(
        [
            terms[i * height : (i + 1) * height, columns:]
            for i in range(1, terms.shape[0] // height)
        ],
        axis=1,
    )
    parts = jnp.concatenate(split3(solved), axis=0)
    return vector_ref[...] - contract(parts, extended_ref[...], 0, 0)


def apply_matrix(vector, matrix_ref, face_refs):
    rounded = vector.astype(bf16)
    padded = matrix_ref.shape[1] // 4
    for slot, face_ref in enumerate(face_refs):
        product = contract(rounded, matrix_ref[:, slot * padded : (slot + 1) * padded], 1, 0)
        face_ref[...] = pack_face(product, face_ref.shape)


def start_kernel(coeff_ref, inverse_ref, extended_ref, vector_ref, matrix_ref, *refs):
    residual_ref, face_refs = refs[0], refs[1:]
    residual = projected(coeff_ref, inverse_ref, extended_ref, vector_ref)
    residual_ref[...] = residual
    apply_matrix(residual, matrix_ref, face_refs)


def residual_kernel(coeff_ref, inverse_ref, extended_ref, vector_ref, matrix_ref, old_ref, *refs):
    residual_ref, face_refs = refs[0], refs[1:]
    residual = old_ref[...] - projected(coeff_ref, inverse_ref, extended_ref, vector_ref)
    residual_ref[...] = residual
    apply_matrix(residual, matrix_ref, face_refs)


def first_direction_kernel(alpha, coeff_ref, inverse_ref, extended_ref, vector_ref, matrix_ref, *refs):
    direction_ref, face_refs = refs[0], refs[1:]
    direction = alpha * projected(coeff_ref, inverse_ref, extended_ref, vector_ref)
    direction_ref[...] = direction
    apply_matrix(direction, matrix_ref, face_refs)


def direction_kernel(
    alpha, beta, coeff_ref, inverse_ref, extended_ref, vector_ref, matrix_ref, old_ref, *refs
):
    multipliers_ref, face_refs = refs[0], refs[1:]
    old = old_ref[...]
    preconditioned = projected(coeff_ref, inverse_ref, extended_ref, vector_ref)
    direction = alpha * preconditioned + beta * old
    multipliers_ref[...] = old + direction
    apply_matrix(direction, matrix_ref, face_refs)


def face_order(value, reorder_ref):
    parity = row_parity()
    padded, width = value.shape[1] // 4, reorder_ref.shape[2]
    slots = [value[:, slot * padded : (slot + 1) * padded] for slot in range(4)]
    faces = []
    for face in range(4):
        block = by_parity(
            parity, slots[EVEN_FACES.index(face)], slots[ODD_FACES.index(face)]
        )
        if face in REORDERED:
            faces.append(reorder_exact(block, reorder_ref[REORDERED.index(face)], 0))
        else:
            faces.append(block[:, :width])
    return jnp.concatenate(faces, axis=1)


def last_kernel(
    coeff_ref, inverse_ref, extended_ref, vector_ref, old_ref, reorder_ref, out_hbm, out_ref, sems
):
    residual = old_ref[...] - projected(coeff_ref, inverse_ref, extended_ref, vector_ref)
    parts = sems.shape[0]
    share = residual.shape[0] // parts
    copies = []
    for i in range(parts):
        out_ref[i] = face_order(residual[i * share : (i + 1) * share], reorder_ref)
        target = out_hbm.at[pl.ds(i * share, share)]
        copies.append(pltpu.make_async_copy(out_ref.at[i], target, sems.at[i]))
        copies[-1].start()
    for copy in copies:
        copy.wait()


def multipliers_kernel(vector_ref, reorder_ref, out_ref):
    out_ref[...] = face_order(vector_ref[...], reorder_ref)


def call(kernel, outs, args, hbm=(), after=(), scratch=(), aliases={}, out_space=pltpu.VMEM):
    vmem = pl.BlockSpec(memory_space=pltpu.VMEM)
    outside = pl.BlockSpec(memory_space=pltpu.HBM)
    anywhere = pl.BlockSpec(memory_space=pl.ANY)
    size = sum(o.size * o.dtype.itemsize for o in (*outs, *args))
    args = [
        pltpu.with_memory_space_constraint(arg, pltpu.HBM) if i in hbm else arg
        for i, arg in enumerate(args)
    ]
    return pl.pallas_call(
        kernel,
        out_shape=tuple(outs),
        in_specs=[
            outside if i in hbm else anywhere if i in after else vmem for i in range(len(args))
        ],
        out_specs=tuple([pl.BlockSpec(memory_space=out_space)] * len(outs)),
        scratch_shapes=list(scratch),
        input_output_aliases=aliases,
        compiler_params=pltpu.CompilerParams(vmem_limit_bytes=min(size + (8 << 20), 56 << 20)),
    )(*args)


def local(rows, cols, load, dual_operator, dirichlet, modes, coarse_inverse, face_counts, partners):
    devices = rows * cols
    columns, slots = load.shape[2:]
    width = partners.shape[3]
    padded = round_up(width, 128)
    count = modes.shape[2]
    group = round_up(count, 8)
    height = round_up(5 * count, 16)
    long, short = pack_counts(count)
    packed = columns + columns // (long // short)
    lists = exchanges(rows, cols)
    shape = jax.ShapeDtypeStruct
    vector = shape((columns, 4 * padded), f32)
    faces = [shape(packed_shape(columns, width, padded), f32)] * 4
    base = columns + group
    lines = inverse_lines(cols, group, rows * count, padded)
    tall_faces = [shape((base + extra, padded), f32) for extra in (0, lines, 0, lines)]
    matrix = shape((4 * padded, 4 * padded), bf16)
    coeff = shape((devices * long, packed), f32)
    result = shape((columns, slots), f32)
    (alpha_0, _), (alpha_1, beta_1) = chebyshev_coefficients()

    def everywhere(values):
        chunks = values.reshape(devices, long, 1, packed)
        return lax.all_to_all(chunks, ("gy", "gx"), 0, 0).reshape(devices * long, packed)

    raw = shape((slots, slots), bf16)
    wide = pltpu.VMEM((slots, 4 * padded), bf16)
    *sent, live, reorder, places, smoother, own_part = call(
        load_kernel,
        [
            *tall_faces,
            shape((8, 4 * padded), f32),
            shape((len(REORDERED), padded, width), bf16),
            shape((rows * count, (1 + long // short) * rows * long), bf16),
            raw,
            shape(coarse_inverse.shape, f32),
        ],
        (load, modes, partners, face_counts, dirichlet, coarse_inverse),
        (0, 1, 2, 3, 4, 5),
        (),
        [
            pltpu.VMEM((columns, slots), f32),
            pltpu.VMEM((count, slots), bf16),
            pltpu.VMEM((4, width), jnp.int32),
            pltpu.SMEM((1, 4), jnp.int32),
            pltpu.SemaphoreType.DMA((6,)),
        ],
    )
    parts = [own_part] + [
        lax.ppermute(coarse_inverse, "gy", [(column_met(b, step, cols), b) for b in range(cols)])
        for step in range(1, cols)
    ]
    (smoother,) = call(operator_kernel, [matrix], (smoother, reorder, live), (), (2,), [wide])
    sent[1], sent[3] = call(
        functools.partial(rows_kernel, count, base),
        [tall_faces[1], tall_faces[3]],
        (sent[1], sent[3], *parts, smoother),
        after=(2 + cols,),
        scratch=[pltpu.VMEM((cols, group, rows * count), f32)],
        aliases={0: 0, 1: 1},
    )
    arrived = exchange(sent, lists)
    (operator,) = call(
        operator_kernel, [matrix], (dual_operator[0, 0], reorder, sent[1]), (), (2,), [wide]
    )
    (inverse,) = call(
        functools.partial(inverse_kernel, count, base),
        [shape(((1 + long // short) * height, len(PRODUCTS) * devices * long), bf16)],
        (sent[1], arrived[1], arrived[3], places, *parts, operator),
        (),
        (4 + cols,),
        [pltpu.VMEM((cols, height, rows * count), f32)],
    )
    current, coeffs, mode_columns, extended = call(
        functools.partial(first_join_kernel, count),
        [vector, coeff, shape((4 * padded, 128), bf16), shape((3 * height, 4 * padded), bf16)],
        (*sent, *arrived, live, inverse),
        (),
        (9,),
        [pltpu.VMEM((height, 4 * padded), f32)],
    )

    def join(sent, *before, last=False):
        arrived = exchange(sent, lists)
        current, coeffs = call(
            functools.partial(join_kernel, count),
            [vector, coeff],
            (*sent, *arrived, live, mode_columns, *before),
            (10,) if last else (),
            (10,),
        )
        return everywhere(coeffs), inverse, extended, current

    residual, *sent = call(
        start_kernel,
        [vector, *faces],
        (everywhere(coeffs), inverse, extended, current, smoother),
    )
    direction, *sent = call(
        functools.partial(first_direction_kernel, alpha_0),
        [vector, *faces],
        (*join(sent), operator),
    )
    residual, *sent = call(
        residual_kernel, [vector, *faces], (*join(sent), smoother, residual)
    )
    multipliers, *sent = call(
        functools.partial(direction_kernel, alpha_1, beta_1),
        [vector, *faces],
        (*join(sent), operator, direction),
    )
    (multipliers,) = call(multipliers_kernel, [result], (multipliers, reorder))
    (residual,) = call(
        last_kernel,
        [result],
        (*join(sent, multipliers, last=True), residual, reorder),
        scratch=[pltpu.VMEM((2, columns // 2, slots), f32), pltpu.SemaphoreType.DMA((2,))],
        out_space=pl.ANY,
    )
    return (multipliers[None, None], residual[None, None])


def solution(mesh):
    return jax.shard_map(
        functools.partial(local, mesh.shape["gx"], mesh.shape["gy"]),
        mesh=mesh,
        in_specs=(
            P("gx", "gy", None, None),
            P("gx", "gy", None, None),
            P("gx", "gy", None, None),
            P("gx", "gy", None, None),
            P("gx", None, "gy", None),
            P("gx", "gy", None),
            P("gx", "gy", None, None),
        ),
        out_specs=(P("gx", "gy", None, None), P("gx", "gy", None, None)),
        check_vma=False,
    )
```
